32 devices in a mesh: psg: 16 (over z, y, x), qry: 2 (over core).
Axes of the slice: x: 2, y: 2, z: 4, core: 2. Of those that a mesh axis runs over, the one named last changes fastest.
Arguments:
- queries: bfloat16 [256, 32, 128], P(('psg', 'qry')), may hold values from -0.59765625 to 0.59765625
- cand_shard: int32 [256, 256, 1], P(('psg', 'qry')), may hold values from 0 to 31; in each aligned block of 256 rows (0 to 255, 256 to 511, ..., all dimensions but the last counted through in order) at most 16 rows name the same one
- cand_local: int32 [256, 256], P(('psg', 'qry')), may hold values from 0 to 63
- passages: bfloat16 [2048, 70, 128], P(('psg', 'qry')), may hold values from -0.59765625 to 0.59765625
- lengths: int32 [2048], P(('psg', 'qry')), may hold values from 8 to 70
Outputs:
- scores: float32 [256, 256], P(('psg', 'qry'))
The draws below stay inside these ranges and needn't reach their ends.
Inputs may be any that keep to these rules, and one draw needn't show every extreme that they name: `cand_shard`: among the 256 candidates of one query no device is named more than 16 times, and some query names some device exactly 16 times; some devices hold far more candidates than others.
All inputs are finite; a program needn't handle non-finite values.
Results may differ from the reference program's by a relative error of at most 0.0003.
Values may be sent and summed in bfloat16 or wider, within the bound.
No kernel may reach another device: no remote copies, remote signals or barrier semaphores. Data moves between devices by JAX's collectives and lax.ppermute only.
A program may use at most 128 MiB of HBM per device.

```python
import math
import jax
import jax.numpy as jnp
import numpy as np
from jax import lax

DIM = 128
QLEN = 32
PLEN = 70
POOL = 256
P_DEV = 64
QCAP = 16
QUERIES = 256
PASSAGES = 2048
N_PSG = 16
N_QRY = 2


def touch_ends(values, rng, smallest, top_value):
    place = [jax.random.randint(jax.random.fold_in(rng, axis), (), 0, length) for axis, length in enumerate(values.shape)]
    main_axis = values.shape.index(max(values.shape))
    neighbour = place[:main_axis] + [(place[main_axis] + 1) % values.shape[main_axis]] + place[main_axis + 1:]
    return values.at[tuple(place)].set(smallest).at[tuple(neighbour)].set(top_value)


def level_of(rng, dims, shards, low, high):
    loudness = 1.0
    for position, shards_of in shards:
        heights = jax.random.uniform(jax.random.fold_in(jax.random.fold_in(rng, 6), position), (shards_of,), jnp.float32, low / len(shards), high / len(shards))
        loudness = loudness * jnp.repeat(jnp.exp(heights), dims[position] // shards_of).reshape((-1,) + (1,) * (len(dims) - 1 - position))
    return loudness


def assign_block(own_key, own, number, rows, number_of, top, limit, lean):
    order = jax.random.permutation(own_key, number_of)
    crowded, usual = shares(number_of, rows * top, limit, lean, True), shares(number_of, rows * top, limit, lean, False)
    places = jnp.arange(number_of)

    def named(sizes, rotation):
        used = int((sizes > 0).sum())
        fixed = max(1, used // 4)
        shifted = fixed + (places - fixed + rotation * (used - fixed)) % max(1, number_of - fixed)
        return jnp.zeros((number_of,), jnp.int32).at[order[jnp.where(places < fixed, places, shifted)]].set(jnp.asarray(sizes, jnp.int32))

    sizes = jnp.where(number % 4 == 0, named(crowded, number // 4), named(usual, number - number // 4 - 1))
    mixed = jax.random.permutation(jax.random.fold_in(own, 3), number_of)
    giver, receiver = mixed[0:number_of // 2 * 2:2], mixed[1:number_of // 2 * 2:2]
    margin = jnp.minimum(sizes[giver] - 1, limit - sizes[receiver]) // 2
    margin = jnp.where((giver == order[0]) | (receiver == order[0]) | (sizes[receiver] == 0), 0, jnp.maximum(margin, 0))
    shifted = jax.random.randint(jax.random.fold_in(own, 4), (number_of // 2,), 0, 1 << 20) % (margin + 1)
    sizes = sizes.at[giver].add(-shifted).at[receiver].add(shifted)
    labels = jnp.searchsorted(jnp.cumsum(sizes), jnp.arange(rows * top), side="right").astype(jnp.int32)
    table = labels.reshape(top, rows).T
    table = table[jax.random.permutation(jax.random.fold_in(own, 1), rows)]
    rotation = jax.random.randint(jax.random.fold_in(own, 2), (rows, 1), 0, top)
    return jnp.take_along_axis(table, (jnp.arange(top)[None, :] + rotation) % top, axis=1)


def shares(amount, total, limit, skew, full):
    loads = [(1 << 20) // math.isqrt(standing ** skew) + 1 for standing in range(1, amount + 1)]
    largest = limit if full else min(limit, max(-(-total // amount), total * loads[0] // sum(loads)))
    least = 1 if total - largest >= amount - 1 else 0
    holding, spare = [largest] + [least] * (amount - 1), total - largest - least * (amount - 1)
    while spare > 0:
        free = [i for i in range(1, amount) if holding[i] < largest] or [i for i in range(1, amount) if holding[i] < limit]
        pool, budget = sum([loads[i] for i in free]), spare
        for i in free:
            more = min(limit - holding[i], max(1, budget * loads[i] // pool), spare)
            holding[i] = holding[i] + more
            spare = spare - more
    return np.array(holding)


def scatter_about(key, shape, width, reach, cuts=(), held_as=jnp.bfloat16):
    array = jax.random.normal(key, shape, jnp.float32) * width
    if len(cuts) > 0:
        array = level_of(key, shape, cuts, -0.22, 0.18) * array
    return jnp.clip(array, min=-reach, max=reach).astype(held_as)


def setup_inputs(seed: int = 0) -> dict:
    arg_keys = jax.random.split(jax.random.key(seed), 6)
    queries = scatter_about(arg_keys[0], (QUERIES, QLEN, DIM), 0.1, 0.59765625, ((0, 32),))
    cand_shard_keys = jax.random.split(jax.random.fold_in(arg_keys[1], 1), QUERIES * POOL // POOL)
    cand_shard_turns = jax.random.permutation(jax.random.fold_in(arg_keys[1], 3), QUERIES * POOL // POOL)
    cand_shard = jax.vmap(lambda own, number: assign_block(jax.random.fold_in(arg_keys[1], 2), own, number, POOL, N_PSG * N_QRY, 1, QCAP, 2))(cand_shard_keys, cand_shard_turns).reshape((QUERIES, POOL, 1))
    cand_local = touch_ends(jax.random.randint(arg_keys[2], (QUERIES, POOL), 0, P_DEV), jax.random.fold_in(arg_keys[2], 1), 0, P_DEV - 1).astype(jnp.int32)
    passages = scatter_about(arg_keys[3], (PASSAGES, PLEN, DIM), 0.1, 0.59765625, ((0, 32),))
    lengths = touch_ends(jax.random.randint(arg_keys[4], (PASSAGES,), PLEN // 8, PLEN + 1), jax.random.fold_in(arg_keys[4], 1), PLEN // 8, PLEN).astype(jnp.int32)
    return {"queries": queries, "cand_shard": cand_shard, "cand_local": cand_local, "passages": passages, "lengths": lengths}


def pair_scores(query_tile_block, passage_tile_block, token_counts):
    token_similarity = jnp.einsum("ajs,aeks->aejk", query_tile_block.astype(jnp.float32), passage_tile_block.astype(jnp.float32))
    positions = jnp.arange(passage_tile_block.shape[2], dtype=jnp.int32)
    valid_tokens = positions[None, None, None, :] < token_counts[:, :, None, None]
    return jnp.sum(jnp.max(jnp.where(valid_tokens, token_similarity, -1e30), axis=3), axis=2)


def reference(queries, cand_shard, cand_local, passages, lengths):
    passage_row = (cand_shard[:, :, 0] * P_DEV + cand_local).astype(jnp.int32)
    block_rows = 8
    block_count = QUERIES // block_rows

    def single_block(tiles):
        query_tile_block, rows_block = tiles
        return pair_scores(query_tile_block, passages[rows_block], lengths[rows_block])

    rescored_output = lax.map(single_block, (queries.reshape(block_count, block_rows, QLEN, DIM), passage_row.reshape(block_count, block_rows, POOL)))
    return rescored_output.reshape(QUERIES, POOL)
```

```python
import functools

import jax
import jax.numpy as jnp
from jax import lax
from jax.experimental import pallas as pl
from jax.experimental.pallas import tpu as pltpu
from jax.sharding import PartitionSpec as P

CONTRACT_LAST = (((1,), (1,)), ((), ()))
VMEM = pl.BlockSpec(memory_space=pltpu.VMEM)
SMEM = pl.BlockSpec(memory_space=pltpu.SMEM)
TOKENS = 32
BLOCKS = 4


def maxsim(rows, own_ref, sib_ref):
    tokens, store, dim = own_ref.shape
    width = 2 * store
    best = None
    for j in range(0, tokens, 2):
        weights = jnp.concatenate(
            [own_ref[j], sib_ref[j], own_ref[j + 1], sib_ref[j + 1]], axis=0
        )
        products = lax.dot_general(
            rows, weights, CONTRACT_LAST, preferred_element_type=jnp.float32
        )
        pair = jnp.maximum(products[:, :width], products[:, width:])
        best = pair if best is None else jnp.maximum(best, pair)
    return best


def score_kernel(ids_ref, own_ref, sib_ref, a_ref, b_ref, table_in_ref, out_ref):
    out_ref[...] = table_in_ref[...]
    blocks, half_rows, dim = a_ref.shape
    step = min(blocks, BLOCKS)
    count = half_rows // TOKENS

    def chunk(start):
        rows = jnp.concatenate(
            [ref[pl.ds(start, step)].reshape(-1, dim) for ref in (a_ref, b_ref)], axis=0
        )
        sums = maxsim(rows, own_ref, sib_ref).reshape(2, step, count, TOKENS, -1).sum(axis=3)
        for part in range(2):
            for k in range(step):
                out_ref[ids_ref[part, start + k], part * count : (part + 1) * count, :] = sums[part, k]

    if blocks == step:
        chunk(0)
    else:
        pl.loop(0, blocks, step=step)(chunk)


def score(me, a_blocks, b_blocks, own, sib, a, b, table):
    ids = me ^ jnp.array([a_blocks, b_blocks], jnp.int32)
    return pl.pallas_call(
        score_kernel,
        out_shape=jax.ShapeDtypeStruct(table.shape, jnp.float32),
        in_specs=[SMEM] + [VMEM] * 5,
        out_specs=VMEM,
        input_output_aliases={5: 0},
        compiler_params=pltpu.CompilerParams(vmem_limit_bytes=48 << 20),
        name="score",
    )(ids, own, sib, a, b, table)


def pick_kernel(core_ref, table_ref, shard_ref, local_ref, out_ref):
    chips, rows, width = table_ref.shape
    store = width // 2
    for half in range(shard_ref.shape[1] // 128):
        lanes = slice(half * 128, half * 128 + 128)
        shard = shard_ref[:, lanes]
        chip = shard // 2
        lane = ((shard % 2) ^ core_ref[0]) * store + local_ref[:, lanes]
        total = jnp.zeros(lane.shape, jnp.float32)
        for k in range(chips):
            found = jnp.take_along_axis(table_ref[k], lane, axis=1)
            total = jnp.where(chip == k, found, total)
        out_ref[:, lanes] = total


def body(queries, cand_shard, cand_local, passages, lengths):
    me = lax.axis_index("psg").astype(jnp.int32)
    core = lax.axis_index("qry").reshape(1).astype(jnp.int32)
    chips = lax.axis_size("psg")
    local, qlen, dim = queries.shape
    store, plen, _ = passages.shape

    def swap(a, bits):
        return lax.ppermute(a, "psg", [(i, i ^ bits) for i in range(chips)])

    valid = jnp.arange(plen)[None, :, None] < lengths[:, None, None]
    own = jnp.where(valid, passages, passages[:, :1]).transpose(1, 0, 2)
    sib = lax.ppermute(own, "qry", [(0, 1), (1, 0)])

    half = local * qlen // 2
    rows = queries.reshape(1, 2, half, dim)
    if chips == 16:
        column = jnp.concatenate([rows] + [swap(rows, z) for z in (4, 8, 12)], axis=0)
    else:
        column, bit = rows, 4
        while bit < chips:
            column = jnp.concatenate([column, swap(column, bit)], axis=0)
            bit *= 2
    near = list(range(0, chips, 4))
    beside = [[n ^ k for n in near] for k in range(4)]
    a, b = column[:, 0], column[:, 1]
    a1, b1 = swap(a, 1), swap(b, 2)
    a2 = swap(jnp.concatenate([a, a1]), 2)
    b2 = swap(jnp.concatenate([b, b1]), 1)
    table = jnp.zeros((chips, local, 2 * store), jnp.float32)
    table = score(me, beside[0], beside[0], own, sib, a, b, table)
    table = score(me, beside[1], beside[2], own, sib, a1, b1, table)
    table = score(me, beside[2] + beside[3], beside[1] + beside[3], own, sib, a2, b2, table)
    returned = lax.all_to_all(table, "psg", split_axis=0, concat_axis=0, tiled=True)
    return pl.pallas_call(
        pick_kernel,
        out_shape=jax.ShapeDtypeStruct(cand_local.shape, jnp.float32),
        in_specs=[SMEM, VMEM, VMEM, VMEM],
        out_specs=VMEM,
        name="pick",
    )(core, returned, cand_shard[:, :, 0], cand_local)


def solution(mesh):
    in_specs = (
        P(("psg", "qry"), None, None),
        P(("psg", "qry"), None, None),
        P(("psg", "qry"), None),
        P(("psg", "qry"), None, None),
        P(("psg", "qry")),
    )
    out_specs = P(("psg", "qry"), None)
    return jax.shard_map(body, mesh=mesh, in_specs=in_specs, out_specs=out_specs, check_vma=False)
```

```python
import functools

import jax
import jax.numpy as jnp
from jax import lax
from jax.experimental import pallas as pl
from jax.experimental.pallas import tpu as pltpu
from jax.sharding import PartitionSpec as P

VMEM = pl.BlockSpec(memory_space=pltpu.VMEM)
SMEM = pl.BlockSpec(memory_space=pltpu.SMEM)
TOKENS = 32
BLOCKS = 4
GROUPS = 2
CHUNK = 8
LANES = 128
LOWEST = -1e30


def prep_kernel(lengths_ref, passages_ref, out_ref):
    slots, store, dim = passages_ref.shape
    padded = out_ref.shape[0] - 2
    per_core = store // GROUPS
    shape = (store, 2 * store)
    along = jnp.broadcast_to(lengths_ref[...], shape)
    row = lax.broadcasted_iota(jnp.int32, shape, 0)
    lane = lax.broadcasted_iota(jnp.int32, shape, 1)
    lane = jnp.where(lane >= store, lane - store, lane)
    down = jnp.sum(jnp.where(lane == row, along, 0), axis=1, keepdims=True) // 2
    longer = (down > along) | ((down == along) & (row < lane))
    rank = jnp.sum(longer.astype(jnp.int32), axis=0, keepdims=True)
    sorted_lengths = jnp.sum(jnp.where(rank == row, along, 0), axis=1, keepdims=True) // 2

    square = (2 * store, 2 * store)
    row = lax.broadcasted_iota(jnp.int32, square, 0)
    lane = lax.broadcasted_iota(jnp.int32, square, 1)
    target = rank + jnp.where(lane >= store, store, 0)
    order = (target == row).astype(jnp.float32).astype(passages_ref.dtype)

    first = None
    for t in range(0, slots, 2):
        pair = passages_ref[t : t + 2].reshape(2 * store, dim)
        moved = jnp.dot(order, pair, preferred_element_type=jnp.float32).reshape(2, store, dim)
        first = moved[0] if first is None else first
        for k in range(2):
            out_ref[t + k] = jnp.where(t + k < sorted_lengths, moved[k], first).astype(out_ref.dtype)
    for t in range(slots, padded):
        out_ref[t] = first.astype(out_ref.dtype)
    place = rank + jnp.where(rank >= per_core, per_core, 0)
    for k, value in enumerate((sorted_lengths, place)):
        value = jnp.broadcast_to(value, (store, dim)).astype(jnp.float32)
        out_ref[padded + k] = value.astype(out_ref.dtype)


def prep(passages, lengths):
    store, slots, dim = passages.shape
    padded = -(-slots // CHUNK) * CHUNK
    return pl.pallas_call(
        prep_kernel,
        out_shape=jax.ShapeDtypeStruct((padded + 2, store, dim), passages.dtype),
        in_specs=[VMEM, VMEM],
        out_specs=VMEM,
        compiler_params=pltpu.CompilerParams(vmem_limit_bytes=12 << 20),
        name="prep",
    )(jnp.tile(lengths, 2).reshape(1, 2 * store), passages.transpose(1, 0, 2))


def chunk_counts(own, sib):
    per_core = own.shape[1] // GROUPS
    longest = [plane[-2, ::per_core, 0].astype(jnp.int32) for plane in (own, sib)]
    return (jnp.maximum(*longest) + CHUNK - 1) // CHUNK


def score_block(own_ref, sib_ref, read_rows, acc, sums, units, counts, write):
    half = acc[0].shape[1]
    per_core = own_ref.shape[1] // GROUPS
    width = 2 * per_core
    per_tile = 2 * LANES // width
    last = counts[0] + counts[1] - 1
    zeros = jnp.zeros((2 * LANES, LANES), own_ref.dtype)

    def where_of(step):
        group = (step >= counts[0]).astype(jnp.int32)
        return group, step - group * counts[0]

    def push(step):
        group, at = where_of(step)
        lanes = pl.ds(pl.multiple_of(group * per_core, per_core), per_core)
        for unit in range(2):
            parts = []
            for k in range(per_tile):
                slot = at * CHUNK + unit * per_tile + k
                parts += [own_ref[slot, lanes, :], sib_ref[slot, lanes, :]]
            tile = jnp.concatenate([jnp.concatenate(parts, axis=0), zeros], axis=1)
            pltpu.matmul_push_rhs(tile, 0, unit, transpose=True)

    def stream(part, load):
        rows = read_rows(part)
        rows = jnp.concatenate([rows, rows], axis=1)
        for unit in range(2):
            pltpu.matmul_acc_lhs(units[part][unit], rows, 0 if load else None)

    def pop(part, step):
        group, at = where_of(step)
        best = jnp.maximum(pltpu.matmul_pop(units[part][0]), pltpu.matmul_pop(units[part][1]))
        acc[part][group] = jnp.maximum(jnp.where(at == 0, LOWEST, acc[part][group]), best)

    push(0)
    stream(0, True)
    push(1)
    pop(0, 0)
    stream(1, False)

    def body(step, _):
        stream(0, True)
        pop(1, step - 1)
        push(step + 1)
        stream(1, False)
        pop(0, step)
        return 0

    lax.fori_loop(1, last, body, 0)
    stream(0, True)
    pop(1, last - 1)
    stream(1, False)
    pop(0, last)
    pop(1, last)

    for part in range(2):
        lane = lax.broadcasted_iota(jnp.int32, (half, LANES), 1) < width
        first, second = [
            jnp.maximum(acc[part][g, :, :LANES], acc[part][g, :, LANES:]) for g in range(GROUPS)
        ]
        turned = pltpu.roll(jnp.where(lane, second, first), width, 1)
        best = jnp.maximum(jnp.where(lane, first, second), turned)
        partial = best.reshape(half // TOKENS, TOKENS // 8, 8, LANES).sum(axis=1)
        sums[part, :] = partial.reshape(half * 8 // TOKENS, LANES)
        total = sums[part, pl.ds(0, half // TOKENS, stride=8), :]
        for k in range(1, 8):
            total = total + sums[part, pl.ds(k, half // TOKENS, stride=8), :]
        write(part, total)


def score_kernel(pieces, counts_ref, *refs):
    if pieces:
        ids_ref, *refs = refs
    own_ref, sib_ref, blocks_ref, *refs = refs
    earlier, (out_ref, acc_0, acc_1, sums) = refs[:pieces], refs[pieces:]
    blocks, rows, dim = blocks_ref.shape
    step = min(blocks, BLOCKS)
    planes, store, _ = own_ref.shape
    per_core = store // GROUPS
    for k, ref in enumerate(earlier):
        for block in range(blocks):
            out_ref[ids_ref[k, block]] = ref[block]

    lane = lax.broadcasted_iota(jnp.int32, (16, LANES), 1)
    position = jnp.where(
        lane < store,
        own_ref[planes - 1, :16].astype(jnp.float32),
        sib_ref[planes - 1, :16].astype(jnp.float32) + per_core,
    ).astype(jnp.int32)[:8]

    def run(*units):
        def chunk(start):
            def read_rows(part):
                return blocks_ref[pl.ds(start + part * (step // 2), step // 2)].reshape(-1, dim)

            def write(part, total):
                count = rows // TOKENS
                for k in range(step // 2):
                    block = start + part * (step // 2) + k
                    picked = jnp.take_along_axis(
                        total[k * count : (k + 1) * count], position, axis=1
                    )
                    out_ref[ids_ref[pieces, block] if pieces else block] = picked

            score_block(
                own_ref, sib_ref, read_rows, (acc_0, acc_1), sums,
                ((units[0], units[1]), (units[2], units[3])), [counts_ref[0], counts_ref[1]], write,
            )

        if blocks == step:
            chunk(0)
        else:
            pl.loop(0, blocks, step=step)(chunk)

    half = step // 2 * rows
    pl.run_scoped(run, *[pltpu.ACC(unit)((half, 2 * LANES), jnp.float32) for unit in (0, 1, 0, 1)])


def score(counts, own, sib, blocks, ids=None, earlier=()):
    count = blocks.shape[0]
    step = min(count, BLOCKS)
    half = step // 2 * blocks.shape[1]
    local = blocks.shape[1] // TOKENS
    scalars = [counts] if ids is None else [counts, ids]
    operands = [own, sib, blocks, *earlier]
    return pl.pallas_call(
        functools.partial(score_kernel, len(earlier)),
        out_shape=jax.ShapeDtypeStruct(
            (count * (1 + len(earlier)), local, 2 * own.shape[1]), jnp.float32
        ),
        in_specs=[SMEM] * len(scalars) + [VMEM] * len(operands),
        out_specs=VMEM,
        scratch_shapes=[
            pltpu.VMEM((GROUPS, half, 2 * LANES), jnp.float32),
            pltpu.VMEM((GROUPS, half, 2 * LANES), jnp.float32),
            pltpu.VMEM((2, half * 8 // TOKENS, LANES), jnp.float32),
        ],
        compiler_params=pltpu.CompilerParams(vmem_limit_bytes=12 << 20),
        cost_estimate=pl.CostEstimate(
            flops=8 * blocks.size * own.shape[0] * own.shape[1],
            bytes_accessed=4 * own.size,
            transcendentals=0,
        ),
        name="score",
    )(*scalars, *operands)


def pick_kernel(core_ref, table_ref, shard_ref, local_ref, out_ref):
    chips, rows, width = table_ref.shape
    store = width // 2
    for half in range(shard_ref.shape[1] // LANES):
        lanes = slice(half * LANES, half * LANES + LANES)
        shard = shard_ref[:, lanes]
        chip = shard // 2
        lane = ((shard % 2) ^ core_ref[0]) * store + local_ref[:, lanes]
        total = jnp.zeros(lane.shape, jnp.float32)
        for k in range(chips):
            found = jnp.take_along_axis(table_ref[k], lane, axis=1)
            total = jnp.where(chip == k, found, total)
        out_ref[:, lanes] = total


def body(queries, cand_shard, cand_local, passages, lengths):
    me = lax.axis_index("psg").astype(jnp.int32)
    core = lax.axis_index("qry").reshape(1).astype(jnp.int32)
    chips = lax.axis_size("psg")
    local, qlen, dim = queries.shape

    def swap(a, bits):
        return lax.ppermute(a, "psg", [(i, i ^ bits) for i in range(chips)])

    rows = queries.reshape(1, local * qlen, dim)
    if chips == 16:
        others = [swap(rows, z) for z in (4, 8, 12)]
        column = jnp.concatenate([rows] + others, axis=0)
    else:
        column, bit = rows, 4
        while bit < chips:
            column = jnp.concatenate([column, swap(column, bit)], axis=0)
            bit *= 2
    own = prep(passages, lengths)
    sib = lax.ppermute(own, "qry", [(0, 1), (1, 0)])
    counts = chunk_counts(own, sib)
    ids = (jnp.arange(0, chips, 4)[None, :] ^ jnp.arange(4)[:, None]).astype(jnp.int32) ^ me
    beside = [column] + [swap(column, k) for k in (1, 2, 3)]
    pieces = [score(counts, own, sib, beside[k]) for k in range(3)]
    table = score(counts, own, sib, beside[3], ids, pieces)
    returned = lax.all_to_all(table, "psg", split_axis=0, concat_axis=0, tiled=True)
    return pl.pallas_call(
        pick_kernel,
        out_shape=jax.ShapeDtypeStruct(cand_local.shape, jnp.float32),
        in_specs=[SMEM, VMEM, VMEM, VMEM],
        out_specs=VMEM,
        compiler_params=pltpu.CompilerParams(vmem_limit_bytes=4 << 20),
        name="pick",
    )(core, returned, cand_shard[:, :, 0], cand_local)


def solution(mesh):
    in_specs = (
        P(("psg", "qry"), None, None),
        P(("psg", "qry"), None, None),
        P(("psg", "qry"), None),
        P(("psg", "qry"), None, None),
        P(("psg", "qry")),
    )
    out_specs = P(("psg", "qry"), None)
    return jax.shard_map(body, mesh=mesh, in_specs=in_specs, out_specs=out_specs, check_vma=False)
```

```python
import functools

import jax
import jax.numpy as jnp
from jax import lax
from jax.experimental import pallas as pl
from jax.experimental.pallas import tpu as pltpu
from jax.sharding import PartitionSpec as P

VMEM = pl.BlockSpec(memory_space=pltpu.VMEM)
SMEM = pl.BlockSpec(memory_space=pltpu.SMEM)
TOKENS = 32
BLOCKS = 4
GROUPS = 2
CHUNK = 8
LANES = 128
ROWS = 128
LOWEST = -1e30


def prep_kernel(counts_ref, store_ref, out_ref, lengths_ref, passages_ref, arrived):
    load_lengths = pltpu.make_async_copy(counts_ref, lengths_ref, arrived.at[0])
    load_store = pltpu.make_async_copy(store_ref, passages_ref, arrived.at[1])
    load_lengths.start()
    load_store.start()
    load_lengths.wait()
    slots, store, dim = passages_ref.shape
    padded = out_ref.shape[0] - 2
    per_core = store // GROUPS
    shape = (store, 2 * store)
    lengths = lengths_ref[...]
    along = jnp.broadcast_to(jnp.concatenate([lengths, lengths], axis=1), shape)
    row = lax.broadcasted_iota(jnp.int32, shape, 0)
    lane = lax.broadcasted_iota(jnp.int32, shape, 1)
    lane = jnp.where(lane >= store, lane - store, lane)
    down = jnp.sum(jnp.where(lane == row, along, 0), axis=1, keepdims=True) // 2
    longer = (down > along) | ((down == along) & (row < lane))
    rank = jnp.sum(longer.astype(jnp.int32), axis=0, keepdims=True)
    sorted_lengths = jnp.sum(jnp.where(rank == row, along, 0), axis=1, keepdims=True) // 2

    square = (2 * store, 2 * store)
    row = lax.broadcasted_iota(jnp.int32, square, 0)
    lane = lax.broadcasted_iota(jnp.int32, square, 1)
    target = rank + jnp.where(lane >= store, store, 0)
    order = (target == row).astype(jnp.float32).astype(passages_ref.dtype)

    load_store.wait()
    first = None
    for t in range(0, slots, 2):
        pair = passages_ref[t : t + 2].reshape(2 * store, dim)
        moved = jnp.dot(order, pair, preferred_element_type=jnp.float32).reshape(2, store, dim)
        first = moved[0] if first is None else first
        for k in range(2):
            out_ref[t + k] = jnp.where(t + k < sorted_lengths, moved[k], first).astype(out_ref.dtype)
    for t in range(slots, padded):
        out_ref[t] = first.astype(out_ref.dtype)
    place = rank + jnp.where(rank >= per_core, per_core, 0)
    for k, value in enumerate((sorted_lengths, place)):
        value = jnp.broadcast_to(value, (store, dim)).astype(jnp.float32)
        out_ref[padded + k] = value.astype(out_ref.dtype)


def prep(passages, lengths):
    store, slots, dim = passages.shape
    padded = -(-slots // CHUNK) * CHUNK
    return pl.pallas_call(
        prep_kernel,
        out_shape=jax.ShapeDtypeStruct((padded + 2, store, dim), passages.dtype),
        in_specs=[pl.BlockSpec(memory_space=pl.ANY)] * 2,
        out_specs=VMEM,
        scratch_shapes=[
            pltpu.VMEM((1, store), jnp.int32),
            pltpu.VMEM((slots, store, dim), passages.dtype),
            pltpu.SemaphoreType.DMA((2,)),
        ],
        compiler_params=pltpu.CompilerParams(vmem_limit_bytes=12 << 20),
        cost_estimate=pl.CostEstimate(
            flops=64 * passages.size * store, bytes_accessed=4 * passages.size, transcendentals=0
        ),
        name="prep",
    )(
        pltpu.with_memory_space_constraint(lengths.reshape(1, store), pltpu.HBM),
        pltpu.with_memory_space_constraint(passages.transpose(1, 0, 2), pltpu.HBM),
    )


def chunk_counts(own, sib):
    per_core = own.shape[1] // GROUPS
    longest = [plane[-2, ::per_core, 0].astype(jnp.int32) for plane in (own, sib)]
    return (jnp.maximum(*longest) + CHUNK - 1) // CHUNK


def score_block(own_ref, sib_ref, read_rows, acc, sums, units, counts, write):
    half = acc[0].shape[1]
    per_core = own_ref.shape[1] // GROUPS
    width = 2 * per_core
    per_tile = 2 * LANES // width
    last = counts[0] + counts[1] - 1
    zeros = jnp.zeros((2 * LANES, LANES), own_ref.dtype)

    def where_of(step):
        group = (step >= counts[0]).astype(jnp.int32)
        return group, step - group * counts[0]

    def push(step):
        group, at = where_of(step)
        lanes = pl.ds(pl.multiple_of(group * per_core, per_core), per_core)
        for unit in range(2):
            parts = []
            for k in range(per_tile):
                slot = at * CHUNK + unit * per_tile + k
                parts += [own_ref[slot, lanes, :], sib_ref[slot, lanes, :]]
            tile = jnp.concatenate([jnp.concatenate(parts, axis=0), zeros], axis=1)
            pltpu.matmul_push_rhs(tile, 0, unit, transpose=True)

    def stream(part, load):
        rows = read_rows(part)
        rows = jnp.concatenate([rows, rows], axis=1)
        for unit in range(2):
            pltpu.matmul_acc_lhs(units[part][unit], rows, 0 if load else None)

    def pop(part, step):
        group, at = where_of(step)
        best = jnp.maximum(pltpu.matmul_pop(units[part][0]), pltpu.matmul_pop(units[part][1]))
        acc[part][group] = jnp.maximum(jnp.where(at == 0, LOWEST, acc[part][group]), best)

    push(0)
    stream(0, True)
    push(1)
    pop(0, 0)
    stream(1, False)

    def body(step, _):
        stream(0, True)
        pop(1, step - 1)
        push(step + 1)
        stream(1, False)
        pop(0, step)
        return 0

    def finish(part):
        _, at = where_of(last)
        fresh = [pltpu.matmul_pop(unit) for unit in units[part]]
        for start in range(0, half, ROWS):
            take = slice(start, start + ROWS)
            best = jnp.maximum(fresh[0][take], fresh[1][take])
            best = jnp.maximum(jnp.where(at == 0, LOWEST, acc[part][GROUPS - 1, take]), best)
            first = acc[part][0, take]
            first = jnp.maximum(first[:, :LANES], first[:, LANES:])
            second = jnp.maximum(best[:, :LANES], best[:, LANES:])
            lane = lax.broadcasted_iota(jnp.int32, first.shape, 1) < width
            turned = pltpu.roll(jnp.where(lane, second, first), width, 1)
            best = jnp.maximum(jnp.where(lane, first, second), turned)
            partial = best.reshape(ROWS // TOKENS, TOKENS // 8, 8, LANES).sum(axis=1)
            spot = start * 8 // TOKENS
            sums[part, spot : spot + ROWS * 8 // TOKENS] = partial.reshape(-1, LANES)
        total = sums[part, pl.ds(0, half // TOKENS, stride=8), :]
        for k in range(1, 8):
            total = total + sums[part, pl.ds(k, half // TOKENS, stride=8), :]
        write(part, total)

    lax.fori_loop(1, last, body, 0)
    stream(0, True)
    pop(1, last - 1)
    stream(1, False)
    finish(0)
    finish(1)


def score_kernel(first, earlier, counts_ref, *refs):
    if earlier:
        ids_ref, *refs = refs
    own_ref, sib_ref, blocks_ref, *refs = refs
    pieces, (out_ref, acc_0, acc_1, sums, scores) = refs[:earlier], refs[earlier:]
    blocks, rows, dim = blocks_ref.shape
    step = min(blocks - first, BLOCKS)
    local = rows // TOKENS
    half = step * rows // 2
    planes, store, _ = own_ref.shape
    per_core = store // GROUPS
    flat_ref = blocks_ref.reshape(blocks * rows, dim)
    at = 0
    for piece in pieces:
        for block in range(piece.shape[0]):
            out_ref[ids_ref[at]] = piece[block]
            at += 1

    lane = lax.broadcasted_iota(jnp.int32, (16, LANES), 1)
    position = jnp.where(
        lane < store,
        own_ref[planes - 1, :16].astype(jnp.float32),
        sib_ref[planes - 1, :16].astype(jnp.float32) + per_core,
    ).astype(jnp.int32)[:1]

    def run(*units):
        def chunk(start):
            def read_rows(part):
                return flat_ref[pl.ds((first + start) * rows + part * half, half)]

            def write(part, total):
                count = half // TOKENS
                index = jnp.broadcast_to(position, (count, LANES))
                scores[part * count : (part + 1) * count] = jnp.take_along_axis(
                    total, index, axis=1
                )

            score_block(
                own_ref, sib_ref, read_rows, (acc_0, acc_1), sums,
                ((units[0], units[1]), (units[2], units[3])), [counts_ref[0], counts_ref[1]], write,
            )
            for block in range(step):
                spot = ids_ref[at + start + block] if earlier else start + block
                out_ref[spot] = scores[block * local : (block + 1) * local]

        if blocks - first == step:
            chunk(0)
        else:
            pl.loop(0, blocks - first, step=step)(chunk)

    pl.run_scoped(run, *[pltpu.ACC(unit)((half, 2 * LANES), jnp.float32) for unit in (0, 1, 0, 1)])


def score(counts, own, sib, blocks, first=0, ids=None, earlier=()):
    count = blocks.shape[0] - first
    step = min(count, BLOCKS)
    half = step * blocks.shape[1] // 2
    local = blocks.shape[1] // TOKENS
    scalars = [counts] if ids is None else [counts, ids]
    operands = [own, sib, blocks, *earlier]
    total = count + sum(piece.shape[0] for piece in earlier)
    return pl.pallas_call(
        functools.partial(score_kernel, first, len(earlier)),
        out_shape=jax.ShapeDtypeStruct((total, local, 2 * own.shape[1]), jnp.float32),
        in_specs=[SMEM] * len(scalars) + [VMEM] * len(operands),
        out_specs=VMEM,
        scratch_shapes=[
            pltpu.VMEM((GROUPS, half, 2 * LANES), jnp.float32),
            pltpu.VMEM((GROUPS, half, 2 * LANES), jnp.float32),
            pltpu.VMEM((2, half * 8 // TOKENS, LANES), jnp.float32),
            pltpu.VMEM((step * local, LANES), jnp.float32),
        ],
        compiler_params=pltpu.CompilerParams(vmem_limit_bytes=12 << 20),
        cost_estimate=pl.CostEstimate(
            flops=8 * count * blocks[0].size * own.shape[0] * own.shape[1],
            bytes_accessed=4 * own.size,
            transcendentals=0,
        ),
        name="score",
    )(*scalars, *operands)


def pick_kernel(core_ref, table_ref, shard_ref, local_ref, out_ref):
    chips, rows, width = table_ref.shape
    store = width // 2
    for half in range(shard_ref.shape[1] // LANES):
        lanes = slice(half * LANES, half * LANES + LANES)
        shard = shard_ref[:, lanes]
        chip = shard // 2
        lane = ((shard % 2) ^ core_ref[0]) * store + local_ref[:, lanes]
        total = jnp.zeros(lane.shape, jnp.float32)
        for k in range(chips):
            found = jnp.take_along_axis(table_ref[k], lane, axis=1)
            total = jnp.where(chip == k, found, total)
        out_ref[:, lanes] = total


def body(queries, cand_shard, cand_local, passages, lengths):
    me = lax.axis_index("psg").astype(jnp.int32)
    core = lax.axis_index("qry").reshape(1).astype(jnp.int32)
    chips = lax.axis_size("psg")
    local, qlen, dim = queries.shape

    def swap(a, bits):
        return lax.ppermute(a, "psg", [(i, i ^ bits) for i in range(chips)])

    own = prep(passages, lengths)
    rows = queries.reshape(1, local * qlen, dim)
    if chips == 16:
        others = [swap(rows, z) for z in (4, 8, 12)]
        own, *others = lax.optimization_barrier((own, *others))
        column = jnp.concatenate([rows] + others, axis=0)
    else:
        column, bit = rows, 4
        while bit < chips:
            column = jnp.concatenate([column, swap(column, bit)], axis=0)
            bit *= 2
    sib = lax.ppermute(own, "qry", [(0, 1), (1, 0)])
    counts = chunk_counts(own, sib)
    ids = (jnp.arange(0, chips, 4)[None, :] ^ jnp.arange(4)[:, None]).astype(jnp.int32) ^ me
    beside = [column] + [swap(column, k) for k in (1, 2, 3)]
    pieces = [score(counts, own, sib, column)]
    pieces += [score(counts, own, sib, beside[k]) for k in (1, 2)]
    table = score(counts, own, sib, beside[3], ids=ids.reshape(-1), earlier=pieces)
    returned = lax.all_to_all(table, "psg", split_axis=0, concat_axis=0, tiled=True)
    return pl.pallas_call(
        pick_kernel,
        out_shape=jax.ShapeDtypeStruct(cand_local.shape, jnp.float32),
        in_specs=[SMEM, VMEM, VMEM, VMEM],
        out_specs=VMEM,
        compiler_params=pltpu.CompilerParams(vmem_limit_bytes=4 << 20),
        name="pick",
    )(core, returned, cand_shard[:, :, 0], cand_local)


def solution(mesh):
    in_specs = (
        P(("psg", "qry"), None, None),
        P(("psg", "qry"), None, None),
        P(("psg", "qry"), None),
        P(("psg", "qry"), None, None),
        P(("psg", "qry")),
    )
    out_specs = P(("psg", "qry"), None)
    return jax.shard_map(body, mesh=mesh, in_specs=in_specs, out_specs=out_specs, check_vma=False)
```

```python
import functools

import jax
import jax.numpy as jnp
from jax import lax
from jax.experimental import pallas as pl
from jax.experimental.pallas import tpu as pltpu
from jax.sharding import PartitionSpec as P

VMEM = pl.BlockSpec(memory_space=pltpu.VMEM)
SMEM = pl.BlockSpec(memory_space=pltpu.SMEM)
TOKENS = 32
BLOCKS = 4
GROUPS = 2
CHUNK = 8
LANES = 128
ROWS = 128
LOWEST = -1e30


def prep_kernel(counts_ref, store_ref, out_ref, lengths_ref, passages_ref, arrived):
    load_lengths = pltpu.make_async_copy(counts_ref, lengths_ref, arrived.at[0])
    load_store = pltpu.make_async_copy(store_ref, passages_ref, arrived.at[1])
    load_lengths.start()
    load_store.start()
    load_lengths.wait()
    slots, store, dim = passages_ref.shape
    padded = out_ref.shape[0] - 2
    per_core = store // GROUPS
    shape = (store, 2 * store)
    lengths = lengths_ref[...]
    along = jnp.broadcast_to(jnp.concatenate([lengths, lengths], axis=1), shape)
    row = lax.broadcasted_iota(jnp.int32, shape, 0)
    lane = lax.broadcasted_iota(jnp.int32, shape, 1)
    lane = jnp.where(lane >= store, lane - store, lane)
    down = jnp.sum(jnp.where(lane == row, along, 0), axis=1, keepdims=True) // 2
    longer = (down > along) | ((down == along) & (row < lane))
    rank = jnp.sum(longer.astype(jnp.int32), axis=0, keepdims=True)
    sorted_lengths = jnp.sum(jnp.where(rank == row, along, 0), axis=1, keepdims=True) // 2

    square = (2 * store, 2 * store)
    row = lax.broadcasted_iota(jnp.int32, square, 0)
    lane = lax.broadcasted_iota(jnp.int32, square, 1)
    target = rank + jnp.where(lane >= store, store, 0)
    order = (target == row).astype(jnp.float32).astype(passages_ref.dtype)

    load_store.wait()
    first = None
    for t in range(0, slots, 2):
        pair = passages_ref[t : t + 2].reshape(2 * store, dim)
        moved = jnp.dot(order, pair, preferred_element_type=jnp.float32).reshape(2, store, dim)
        first = moved[0] if first is None else first
        for k in range(2):
            out_ref[t + k] = jnp.where(t + k < sorted_lengths, moved[k], first).astype(out_ref.dtype)
    for t in range(slots, padded):
        out_ref[t] = first.astype(out_ref.dtype)
    place = rank + jnp.where(rank >= per_core, per_core, 0)
    for k, value in enumerate((sorted_lengths, place)):
        value = jnp.broadcast_to(value, (store, dim)).astype(jnp.float32)
        out_ref[padded + k] = value.astype(out_ref.dtype)


def prep(passages, lengths):
    store, slots, dim = passages.shape
    padded = -(-slots // CHUNK) * CHUNK
    return pl.pallas_call(
        prep_kernel,
        out_shape=jax.ShapeDtypeStruct((padded + 2, store, dim), passages.dtype),
        in_specs=[pl.BlockSpec(memory_space=pl.ANY)] * 2,
        out_specs=VMEM,
        scratch_shapes=[
            pltpu.VMEM((1, store), jnp.int32),
            pltpu.VMEM((slots, store, dim), passages.dtype),
            pltpu.SemaphoreType.DMA((2,)),
        ],
        compiler_params=pltpu.CompilerParams(vmem_limit_bytes=12 << 20),
        cost_estimate=pl.CostEstimate(
            flops=64 * passages.size * store, bytes_accessed=4 * passages.size, transcendentals=0
        ),
        name="prep",
    )(
        pltpu.with_memory_space_constraint(lengths.reshape(1, store), pltpu.HBM),
        pltpu.with_memory_space_constraint(passages.transpose(1, 0, 2), pltpu.HBM),
    )


def chunk_counts(own, sib):
    per_core = own.shape[1] // GROUPS
    longest = [plane[-2, ::per_core, 0].astype(jnp.int32) for plane in (own, sib)]
    return (jnp.maximum(*longest) + CHUNK - 1) // CHUNK


def score_block(own_ref, sib_ref, read_rows, acc, sums, units, counts, write):
    half = acc[0].shape[1]
    per_core = own_ref.shape[1] // GROUPS
    width = 2 * per_core
    per_tile = 2 * LANES // width
    last = counts[0] + counts[1] - 1
    zeros = jnp.zeros((2 * LANES, LANES), own_ref.dtype)

    def where_of(step):
        group = (step >= counts[0]).astype(jnp.int32)
        return group, step - group * counts[0]

    def push(step):
        group, at = where_of(step)
        lanes = pl.ds(pl.multiple_of(group * per_core, per_core), per_core)
        for unit in range(2):
            parts = []
            for k in range(per_tile):
                slot = at * CHUNK + unit * per_tile + k
                parts += [own_ref[slot, lanes, :], sib_ref[slot, lanes, :]]
            tile = jnp.concatenate([jnp.concatenate(parts, axis=0), zeros], axis=1)
            pltpu.matmul_push_rhs(tile, 0, unit, transpose=True)

    def stream(part, load):
        rows = read_rows(part)
        rows = jnp.concatenate([rows, jnp.zeros_like(rows)], axis=1)
        for unit in range(2):
            pltpu.matmul_acc_lhs(units[part][unit], rows, 0 if load else None)

    def pop(part, step):
        group, at = where_of(step)
        best = jnp.maximum(pltpu.matmul_pop(units[part][0]), pltpu.matmul_pop(units[part][1]))
        acc[part][group] = jnp.maximum(jnp.where(at == 0, LOWEST, acc[part][group]), best)

    push(0)
    stream(0, True)
    push(1)
    pop(0, 0)
    stream(1, False)

    def body(step, _):
        stream(0, True)
        pop(1, step - 1)
        push(step + 1)
        stream(1, False)
        pop(0, step)
        return 0

    def finish(part):
        _, at = where_of(last)
        fresh = [pltpu.matmul_pop(unit) for unit in units[part]]
        for start in range(0, half, ROWS):
            take = slice(start, start + ROWS)
            best = jnp.maximum(fresh[0][take], fresh[1][take])
            best = jnp.maximum(jnp.where(at == 0, LOWEST, acc[part][GROUPS - 1, take]), best)
            first = acc[part][0, take]
            first = jnp.maximum(first[:, :LANES], first[:, LANES:])
            second = jnp.maximum(best[:, :LANES], best[:, LANES:])
            lane = lax.broadcasted_iota(jnp.int32, first.shape, 1) < width
            turned = pltpu.roll(jnp.where(lane, second, first), width, 1)
            best = jnp.maximum(jnp.where(lane, first, second), turned)
            partial = best.reshape(ROWS // TOKENS, TOKENS // 8, 8, LANES).sum(axis=1)
            spot = start * 8 // TOKENS
            sums[part, spot : spot + ROWS * 8 // TOKENS] = partial.reshape(-1, LANES)
        total = sums[part, pl.ds(0, half // TOKENS, stride=8), :]
        for k in range(1, 8):
            total = total + sums[part, pl.ds(k, half // TOKENS, stride=8), :]
        write(part, total)

    lax.fori_loop(1, last, body, 0)
    stream(0, True)
    pop(1, last - 1)
    stream(1, False)
    finish(0)
    finish(1)


def score_kernel(first, earlier, counts_ref, *refs):
    if earlier:
        ids_ref, *refs = refs
    own_ref, sib_ref, blocks_ref, *refs = refs
    pieces, (out_ref, acc_0, acc_1, sums, scores) = refs[:earlier], refs[earlier:]
    blocks, rows, dim = blocks_ref.shape
    step = min(blocks - first, BLOCKS)
    local = rows // TOKENS
    half = step * rows // 2
    planes, store, _ = own_ref.shape
    per_core = store // GROUPS
    flat_ref = blocks_ref.reshape(blocks * rows, dim)
    at = 0
    for piece in pieces:
        for block in range(piece.shape[0]):
            out_ref[ids_ref[at]] = piece[block]
            at += 1

    lane = lax.broadcasted_iota(jnp.int32, (16, LANES), 1)
    position = jnp.where(
        lane < store,
        own_ref[planes - 1, :16].astype(jnp.float32),
        sib_ref[planes - 1, :16].astype(jnp.float32) + per_core,
    ).astype(jnp.int32)[:1]

    def run(*units):
        def chunk(start):
            def read_rows(part):
                return flat_ref[pl.ds((first + start) * rows + part * half, half)]

            def write(part, total):
                count = half // TOKENS
                index = jnp.broadcast_to(position, (count, LANES))
                scores[part * count : (part + 1) * count] = jnp.take_along_axis(
                    total, index, axis=1
                )

            score_block(
                own_ref, sib_ref, read_rows, (acc_0, acc_1), sums,
                ((units[0], units[1]), (units[2], units[3])), [counts_ref[0], counts_ref[1]], write,
            )
            for block in range(step):
                spot = ids_ref[at + start + block] if earlier else start + block
                out_ref[spot] = scores[block * local : (block + 1) * local]

        if blocks - first == step:
            chunk(0)
        else:
            pl.loop(0, blocks - first, step=step)(chunk)

    pl.run_scoped(run, *[pltpu.ACC(unit)((half, 2 * LANES), jnp.float32) for unit in (0, 1, 0, 1)])


def score(counts, own, sib, blocks, first=0, ids=None, earlier=()):
    count = blocks.shape[0] - first
    step = min(count, BLOCKS)
    half = step * blocks.shape[1] // 2
    local = blocks.shape[1] // TOKENS
    scalars = [counts] if ids is None else [counts, ids]
    operands = [own, sib, blocks, *earlier]
    total = count + sum(piece.shape[0] for piece in earlier)
    return pl.pallas_call(
        functools.partial(score_kernel, first, len(earlier)),
        out_shape=jax.ShapeDtypeStruct((total, local, 2 * own.shape[1]), jnp.float32),
        in_specs=[SMEM] * len(scalars) + [VMEM] * len(operands),
        out_specs=VMEM,
        scratch_shapes=[
            pltpu.VMEM((GROUPS, half, 2 * LANES), jnp.float32),
            pltpu.VMEM((GROUPS, half, 2 * LANES), jnp.float32),
            pltpu.VMEM((2, half * 8 // TOKENS, LANES), jnp.float32),
            pltpu.VMEM((step * local, LANES), jnp.float32),
        ],
        compiler_params=pltpu.CompilerParams(vmem_limit_bytes=12 << 20),
        cost_estimate=pl.CostEstimate(
            flops=8 * count * blocks[0].size * own.shape[0] * own.shape[1],
            bytes_accessed=4 * own.size,
            transcendentals=0,
        ),
        name="score",
    )(*scalars, *operands)


def pick_kernel(core_ref, table_ref, shard_ref, local_ref, out_ref):
    chips, rows, width = table_ref.shape
    store = width // 2
    for half in range(shard_ref.shape[1] // LANES):
        lanes = slice(half * LANES, half * LANES + LANES)
        shard = shard_ref[:, lanes]
        chip = chips - 1 - shard // 2
        lane = ((shard % 2) ^ core_ref[0]) * store + local_ref[:, lanes]
        total = jnp.zeros(lane.shape, jnp.float32)
        for k in range(chips):
            found = jnp.take_along_axis(table_ref[k], lane, axis=1)
            total = jnp.where(chip == k, found, total)
        out_ref[:, lanes] = total


def body(queries, cand_shard, cand_local, passages, lengths):
    me = lax.axis_index("psg").astype(jnp.int32)
    core = lax.axis_index("qry").reshape(1).astype(jnp.int32)
    chips = lax.axis_size("psg")
    local, qlen, dim = queries.shape

    def swap(a, bits):
        return lax.ppermute(a, "psg", [(i, i ^ bits) for i in range(chips)])

    own = prep(passages, lengths)
    rows = queries.reshape(1, local * qlen, dim)
    if chips == 16:
        others = [swap(rows, z) for z in (4, 8, 12)]
        own, *others = lax.optimization_barrier((own, *others))
        column = jnp.concatenate([rows] + others, axis=0)
    else:
        column, bit = rows, 4
        while bit < chips:
            column = jnp.concatenate([column, swap(column, bit)], axis=0)
            bit *= 2
    sib = lax.ppermute(own, "qry", [(0, 1), (1, 0)])
    counts = chunk_counts(own, sib)
    ids = (jnp.arange(0, chips, 4)[None, :] ^ jnp.arange(4)[:, None]).astype(jnp.int32) ^ me
    beside = [column] + [swap(column, k) for k in (1, 2, 3)]
    pieces = [score(counts, own, sib, column)]
    pieces += [score(counts, own, sib, beside[k]) for k in (1, 2)]
    ids = chips - 1 - ids.reshape(-1)
    table = score(counts, own, sib, beside[3], ids=ids, earlier=pieces)
    returned = lax.all_to_all(
        table, "psg", split_axis=0, concat_axis=0, tiled=True,
        axis_index_groups=[list(reversed(range(chips)))],
    )
    return pl.pallas_call(
        pick_kernel,
        out_shape=jax.ShapeDtypeStruct(cand_local.shape, jnp.float32),
        in_specs=[SMEM, VMEM, VMEM, VMEM],
        out_specs=VMEM,
        compiler_params=pltpu.CompilerParams(vmem_limit_bytes=4 << 20),
        name="pick",
    )(core, returned, cand_shard[:, :, 0], cand_local)


def solution(mesh):
    in_specs = (
        P(("psg", "qry"), None, None),
        P(("psg", "qry"), None, None),
        P(("psg", "qry"), None),
        P(("psg", "qry"), None, None),
        P(("psg", "qry")),
    )
    out_specs = P(("psg", "qry"), None)
    return jax.shard_map(body, mesh=mesh, in_specs=in_specs, out_specs=out_specs, check_vma=False)
```

```python
import functools

import jax
import jax.numpy as jnp
from jax import lax
from jax.experimental import pallas as pl
from jax.experimental.pallas import tpu as pltpu
from jax.sharding import PartitionSpec as P

VMEM = pl.BlockSpec(memory_space=pltpu.VMEM)
SMEM = pl.BlockSpec(memory_space=pltpu.SMEM)
TOKENS = 32
BLOCKS = 4
GROUPS = 2
CHUNK = 8
LANES = 128
ROWS = 128
LOWEST = -1e30


def prep_kernel(counts_ref, store_ref, out_ref, lengths_ref, passages_ref, arrived):
    load_lengths = pltpu.make_async_copy(counts_ref, lengths_ref, arrived.at[0])
    load_store = pltpu.make_async_copy(store_ref, passages_ref, arrived.at[1])
    load_lengths.start()
    load_store.start()
    load_lengths.wait()
    slots, store, dim = passages_ref.shape
    padded = out_ref.shape[0] - 2
    per_core = store // GROUPS
    shape = (store, 2 * store)
    lengths = lengths_ref[...]
    along = jnp.broadcast_to(jnp.concatenate([lengths, lengths], axis=1), shape)
    row = lax.broadcasted_iota(jnp.int32, shape, 0)
    lane = lax.broadcasted_iota(jnp.int32, shape, 1)
    lane = jnp.where(lane >= store, lane - store, lane)
    down = jnp.sum(jnp.where(lane == row, along, 0), axis=1, keepdims=True) // 2
    longer = (down > along) | ((down == along) & (row < lane))
    rank = jnp.sum(longer.astype(jnp.int32), axis=0, keepdims=True)
    sorted_lengths = jnp.sum(jnp.where(rank == row, along, 0), axis=1, keepdims=True) // 2

    square = (2 * store, 2 * store)
    row = lax.broadcasted_iota(jnp.int32, square, 0)
    lane = lax.broadcasted_iota(jnp.int32, square, 1)
    target = rank + jnp.where(lane >= store, store, 0)
    order = (target == row).astype(jnp.float32).astype(passages_ref.dtype)

    load_store.wait()
    first = None
    for t in range(0, slots, 2):
        pair = passages_ref[t : t + 2].reshape(2 * store, dim)
        moved = jnp.dot(order, pair, preferred_element_type=jnp.float32).reshape(2, store, dim)
        first = moved[0] if first is None else first
        for k in range(2):
            out_ref[t + k] = jnp.where(t + k < sorted_lengths, moved[k], first).astype(out_ref.dtype)
    for t in range(slots, padded):
        out_ref[t] = first.astype(out_ref.dtype)
    place = rank + jnp.where(rank >= per_core, per_core, 0)
    for k, value in enumerate((sorted_lengths, place)):
        value = jnp.broadcast_to(value, (store, dim)).astype(jnp.float32)
        out_ref[padded + k] = value.astype(out_ref.dtype)


def prep(passages, lengths):
    store, slots, dim = passages.shape
    padded = -(-slots // CHUNK) * CHUNK
    return pl.pallas_call(
        prep_kernel,
        out_shape=jax.ShapeDtypeStruct((padded + 2, store, dim), passages.dtype),
        in_specs=[pl.BlockSpec(memory_space=pl.ANY)] * 2,
        out_specs=VMEM,
        scratch_shapes=[
            pltpu.VMEM((1, store), jnp.int32),
            pltpu.VMEM((slots, store, dim), passages.dtype),
            pltpu.SemaphoreType.DMA((2,)),
        ],
        compiler_params=pltpu.CompilerParams(vmem_limit_bytes=12 << 20),
        cost_estimate=pl.CostEstimate(
            flops=64 * passages.size * store, bytes_accessed=4 * passages.size, transcendentals=0
        ),
        name="prep",
    )(
        pltpu.with_memory_space_constraint(lengths.reshape(1, store), pltpu.HBM),
        pltpu.with_memory_space_constraint(passages.transpose(1, 0, 2), pltpu.HBM),
    )


def chunk_counts(own, sib):
    per_core = own.shape[1] // GROUPS
    longest = [plane[-2, ::per_core, 0].astype(jnp.int32) for plane in (own, sib)]
    return jnp.maximum((jnp.maximum(*longest) + CHUNK - 1) // CHUNK, 2)


def score_block(own_ref, sib_ref, read_rows, acc, sums, units, read_counts, write):
    half = acc[0].shape[1]
    per_core = own_ref.shape[1] // GROUPS
    width = 2 * per_core
    per_tile = 2 * LANES // width
    zeros = jnp.zeros((2 * LANES, LANES), own_ref.dtype)

    def where_of(step):
        if isinstance(step, int):
            return 0, step
        group = (step >= counts[0]).astype(jnp.int32)
        return group, step - group * counts[0]

    def push(step):
        group, at = where_of(step)
        lanes = group * per_core
        lanes = pl.ds(lanes if isinstance(group, int) else pl.multiple_of(lanes, per_core), per_core)
        for unit in range(2):
            parts = []
            for k in range(per_tile):
                slot = at * CHUNK + unit * per_tile + k
                parts += [own_ref[slot, lanes, :], sib_ref[slot, lanes, :]]
            tile = jnp.concatenate([jnp.concatenate(parts, axis=0), zeros], axis=1)
            pltpu.matmul_push_rhs(tile, 0, unit, transpose=True)

    def stream(part, load):
        rows = read_rows(part)
        rows = jnp.concatenate([rows, jnp.zeros_like(rows)], axis=1)
        for unit in range(2):
            pltpu.matmul_acc_lhs(units[part][unit], rows, 0 if load else None)

    def pop(part, step):
        group, at = where_of(step)
        best = jnp.maximum(pltpu.matmul_pop(units[part][0]), pltpu.matmul_pop(units[part][1]))
        if isinstance(step, int):
            acc[part][group] = best if at == 0 else jnp.maximum(acc[part][group], best)
        else:
            acc[part][group] = jnp.maximum(jnp.where(at == 0, LOWEST, acc[part][group]), best)

    push(0)
    stream(0, True)
    push(1)
    pop(0, 0)
    stream(1, False)
    pop(1, 0)
    counts = read_counts()
    last = counts[0] + counts[1] - 1
    stream(0, True)
    push(jnp.minimum(last, 2))
    stream(1, False)
    pop(0, 1)

    def body(step, _):
        stream(0, True)
        pop(1, step - 1)
        push(step + 1)
        stream(1, False)
        pop(0, step)
        return 0

    def finish(part):
        _, at = where_of(last)
        fresh = [pltpu.matmul_pop(unit) for unit in units[part]]
        for start in range(0, half, ROWS):
            take = slice(start, start + ROWS)
            best = jnp.maximum(fresh[0][take], fresh[1][take])
            best = jnp.maximum(jnp.where(at == 0, LOWEST, acc[part][GROUPS - 1, take]), best)
            first = acc[part][0, take]
            first = jnp.maximum(first[:, :LANES], first[:, LANES:])
            second = jnp.maximum(best[:, :LANES], best[:, LANES:])
            lane = lax.broadcasted_iota(jnp.int32, first.shape, 1) < width
            turned = pltpu.roll(jnp.where(lane, second, first), width, 1)
            best = jnp.maximum(jnp.where(lane, first, second), turned)
            partial = best.reshape(ROWS // TOKENS, TOKENS // 8, 8, LANES).sum(axis=1)
            spot = start * 8 // TOKENS
            sums[part, spot : spot + ROWS * 8 // TOKENS] = partial.reshape(-1, LANES)
        total = sums[part, pl.ds(0, half // TOKENS, stride=8), :]
        for k in range(1, 8):
            total = total + sums[part, pl.ds(k, half // TOKENS, stride=8), :]
        write(part, total)

    lax.fori_loop(2, last, body, 0)
    stream(0, True)
    pop(1, last - 1)
    stream(1, False)
    finish(0)
    finish(1)


def score_kernel(first, earlier, counts_ref, *refs):
    if earlier:
        ids_ref, *refs = refs
    own_ref, sib_ref, blocks_ref, *refs = refs
    pieces, refs = refs[:earlier], refs[earlier:]
    out_ref, acc_0, acc_1, sums, scores, counts_here, ids_here, arrived = refs
    load_counts = pltpu.make_async_copy(counts_ref, counts_here, arrived.at[0])
    load_counts.start()
    if earlier:
        load_ids = pltpu.make_async_copy(ids_ref, ids_here, arrived.at[1])
        load_ids.start()
    blocks, rows, dim = blocks_ref.shape
    step = min(blocks - first, BLOCKS)
    local = rows // TOKENS
    half = step * rows // 2
    planes, store, _ = own_ref.shape
    per_core = store // GROUPS
    flat_ref = blocks_ref.reshape(blocks * rows, dim)
    at = sum(piece.shape[0] for piece in pieces)
    waited, placed = [], []

    def receive():
        if placed:
            return
        placed.append(load_ids.wait())
        spot = 0
        for piece in pieces:
            for block in range(piece.shape[0]):
                out_ref[ids_here[spot]] = piece[block]
                spot += 1

    def read_counts():
        if not waited:
            waited.append(load_counts.wait())
        return [counts_here[g] for g in range(GROUPS)]

    lane = lax.broadcasted_iota(jnp.int32, (16, LANES), 1)
    position = jnp.where(
        lane < store,
        own_ref[planes - 1, :16].astype(jnp.float32),
        sib_ref[planes - 1, :16].astype(jnp.float32) + per_core,
    ).astype(jnp.int32)[:1]

    def run(*units):
        def chunk(start):
            def read_rows(part):
                return flat_ref[pl.ds((first + start) * rows + part * half, half)]

            def write(part, total):
                count = half // TOKENS
                index = jnp.broadcast_to(position, (count, LANES))
                scores[part * count : (part + 1) * count] = jnp.take_along_axis(
                    total, index, axis=1
                )

            score_block(
                own_ref, sib_ref, read_rows, (acc_0, acc_1), sums,
                ((units[0], units[1]), (units[2], units[3])), read_counts, write,
            )
            if earlier:
                receive()
            for block in range(step):
                spot = ids_here[at + start + block] if earlier else start + block
                out_ref[spot] = scores[block * local : (block + 1) * local]

        if blocks - first == step:
            chunk(0)
        else:
            read_counts()
            if earlier:
                receive()
            pl.loop(0, blocks - first, step=step)(chunk)

    pl.run_scoped(run, *[pltpu.ACC(unit)((half, 2 * LANES), jnp.float32) for unit in (0, 1, 0, 1)])


def score(counts, own, sib, blocks, first=0, ids=None, earlier=()):
    count = blocks.shape[0] - first
    step = min(count, BLOCKS)
    half = step * blocks.shape[1] // 2
    local = blocks.shape[1] // TOKENS
    scalars = [counts] if ids is None else [counts, ids]
    operands = [own, sib, blocks, *earlier]
    total = count + sum(piece.shape[0] for piece in earlier)
    return pl.pallas_call(
        functools.partial(score_kernel, first, len(earlier)),
        out_shape=jax.ShapeDtypeStruct((total, local, 2 * own.shape[1]), jnp.float32),
        in_specs=[pl.BlockSpec(memory_space=pl.ANY)] * len(scalars) + [VMEM] * len(operands),
        out_specs=VMEM,
        scratch_shapes=[
            pltpu.VMEM((GROUPS, half, 2 * LANES), jnp.float32),
            pltpu.VMEM((GROUPS, half, 2 * LANES), jnp.float32),
            pltpu.VMEM((2, half * 8 // TOKENS, LANES), jnp.float32),
            pltpu.VMEM((step * local, LANES), jnp.float32),
            pltpu.SMEM(counts.shape, jnp.int32),
            pltpu.SMEM((total,), jnp.int32),
            pltpu.SemaphoreType.DMA((2,)),
        ],
        compiler_params=pltpu.CompilerParams(vmem_limit_bytes=12 << 20),
        cost_estimate=pl.CostEstimate(
            flops=8 * count * blocks[0].size * own.shape[0] * own.shape[1],
            bytes_accessed=4 * own.size,
            transcendentals=0,
        ),
        name="score",
    )(*scalars, *operands)


def pick_kernel(core_ref, table_ref, shard_ref, local_ref, out_ref):
    chips, rows, width = table_ref.shape
    store = width // 2
    for half in range(shard_ref.shape[1] // LANES):
        lanes = slice(half * LANES, half * LANES + LANES)
        shard = shard_ref[:, lanes]
        chip = chips - 1 - shard // 2
        lane = ((shard % 2) ^ core_ref[0]) * store + local_ref[:, lanes]
        total = jnp.zeros(lane.shape, jnp.float32)
        for k in range(chips):
            found = jnp.take_along_axis(table_ref[k], lane, axis=1)
            total = jnp.where(chip == k, found, total)
        out_ref[:, lanes] = total


def body(queries, cand_shard, cand_local, passages, lengths):
    me = lax.axis_index("psg").astype(jnp.int32)
    core = lax.axis_index("qry").reshape(1).astype(jnp.int32)
    chips = lax.axis_size("psg")
    local, qlen, dim = queries.shape

    def swap(a, bits):
        return lax.ppermute(a, "psg", [(i, i ^ bits) for i in range(chips)])

    own = prep(passages, lengths)
    rows = queries.reshape(1, local * qlen, dim)
    if chips == 16:
        others = [swap(rows, z) for z in (4, 8, 12)]
        own, *others = lax.optimization_barrier((own, *others))
        column = jnp.concatenate([rows] + others, axis=0)
    else:
        column, bit = rows, 4
        while bit < chips:
            column = jnp.concatenate([column, swap(column, bit)], axis=0)
            bit *= 2
    sib = lax.ppermute(own, "qry", [(0, 1), (1, 0)])
    counts = chunk_counts(own, sib)
    ids = (jnp.arange(0, chips, 4)[None, :] ^ jnp.arange(4)[:, None]).astype(jnp.int32) ^ me
    beside = [column] + [swap(column, k) for k in (1, 2, 3)]
    pieces = [score(counts, own, sib, column)]
    pieces += [score(counts, own, sib, beside[k]) for k in (1, 2)]
    ids = chips - 1 - ids.reshape(-1)
    table = score(counts, own, sib, beside[3], ids=ids, earlier=pieces)
    returned = lax.all_to_all(
        table, "psg", split_axis=0, concat_axis=0, tiled=True,
        axis_index_groups=[list(reversed(range(chips)))],
    )
    return pl.pallas_call(
        pick_kernel,
        out_shape=jax.ShapeDtypeStruct(cand_local.shape, jnp.float32),
        in_specs=[SMEM, VMEM, VMEM, VMEM],
        out_specs=VMEM,
        compiler_params=pltpu.CompilerParams(vmem_limit_bytes=4 << 20),
        name="pick",
    )(core, returned, cand_shard[:, :, 0], cand_local)


def solution(mesh):
    in_specs = (
        P(("psg", "qry"), None, None),
        P(("psg", "qry"), None, None),
        P(("psg", "qry"), None),
        P(("psg", "qry"), None, None),
        P(("psg", "qry")),
    )
    out_specs = P(("psg", "qry"), None)
    return jax.shard_map(body, mesh=mesh, in_specs=in_specs, out_specs=out_specs, check_vma=False)
```

```python
import functools

import jax
import jax.numpy as jnp
from jax import lax
from jax.experimental import pallas as pl
from jax.experimental.pallas import tpu as pltpu
from jax.sharding import PartitionSpec as P

VMEM = pl.BlockSpec(memory_space=pltpu.VMEM)
SMEM = pl.BlockSpec(memory_space=pltpu.SMEM)
TOKENS = 32
BLOCKS = 4
GROUPS = 3
CHUNK = 8
LANES = 128
ROWS = 128
LOWEST = -1e30


def prep_kernel(counts_ref, store_ref, out_ref, lengths_ref, passages_ref, arrived):
    load_lengths = pltpu.make_async_copy(counts_ref, lengths_ref, arrived.at[0])
    load_store = pltpu.make_async_copy(store_ref, passages_ref, arrived.at[1])
    load_lengths.start()
    load_store.start()
    load_lengths.wait()
    slots, store, dim = passages_ref.shape
    quarter = store // 4
    shape = (store, 2 * store)
    lengths = lengths_ref[...]
    along = jnp.broadcast_to(jnp.concatenate([lengths, lengths], axis=1), shape)
    row = lax.broadcasted_iota(jnp.int32, shape, 0)
    lane = lax.broadcasted_iota(jnp.int32, shape, 1)
    lane = jnp.where(lane >= store, lane - store, lane)
    down = jnp.sum(jnp.where(lane == row, along, 0), axis=1, keepdims=True) // 2
    longer = (down > along) | ((down == along) & (row < lane))
    rank = jnp.sum(longer.astype(jnp.int32), axis=0, keepdims=True)
    sorted_lengths = jnp.sum(jnp.where(rank == row, along, 0), axis=1, keepdims=True) // 2

    square = (2 * store, 2 * store)
    row = lax.broadcasted_iota(jnp.int32, square, 0)
    lane = lax.broadcasted_iota(jnp.int32, square, 1)
    target = rank + jnp.where(lane >= store, store, 0)
    order = (target == row).astype(jnp.float32).astype(passages_ref.dtype)

    load_store.wait()
    first = None
    for t in range(0, slots, 2):
        pair = passages_ref[t : t + 2].reshape(2 * store, dim)
        moved = jnp.dot(order, pair, preferred_element_type=jnp.float32).reshape(2, store, dim)
        first = moved[0] if first is None else first
        for k in range(2):
            out_ref[t + k] = jnp.where(t + k < sorted_lengths, moved[k], first).astype(out_ref.dtype)
    place = rank // quarter
    place = jnp.where(place == 0, 3, jnp.where(place == 1, 1, jnp.where(place == 2, 0, 2)))
    place = place * 2 * quarter + rank % quarter
    for k, value in enumerate((sorted_lengths, place)):
        value = jnp.broadcast_to(value, (store, dim)).astype(jnp.float32)
        out_ref[slots + k] = value.astype(out_ref.dtype)


def prep(passages, lengths):
    store, slots, dim = passages.shape
    return pl.pallas_call(
        prep_kernel,
        out_shape=jax.ShapeDtypeStruct((slots + 2, store, dim), passages.dtype),
        in_specs=[pl.BlockSpec(memory_space=pl.ANY)] * 2,
        out_specs=VMEM,
        scratch_shapes=[
            pltpu.VMEM((1, store), jnp.int32),
            pltpu.VMEM((slots, store, dim), passages.dtype),
            pltpu.SemaphoreType.DMA((2,)),
        ],
        compiler_params=pltpu.CompilerParams(vmem_limit_bytes=4 << 20),
        cost_estimate=pl.CostEstimate(
            flops=64 * passages.size * store, bytes_accessed=4 * passages.size, transcendentals=0
        ),
        name="prep",
    )(
        pltpu.with_memory_space_constraint(lengths.reshape(1, store), pltpu.HBM),
        pltpu.with_memory_space_constraint(passages.transpose(1, 0, 2), pltpu.HBM),
    )


def chunk_counts(own, sib):
    quarter = own.shape[1] // 4
    longest = [plane[-2, ::quarter, 0].astype(jnp.int32) for plane in (own, sib)]
    at_once = CHUNK * (1 + jnp.arange(4, dtype=jnp.int32) // 2)
    counts = (jnp.maximum(*longest) + at_once - 1) // at_once
    return jnp.maximum(counts, 2)


def score_block(own_ref, sib_ref, read_rows, acc, sums, units, read_counts, write):
    half = acc[0].shape[1]
    slots = own_ref.shape[0] - 2
    quarter = own_ref.shape[1] // 4
    width = 2 * quarter
    zeros = jnp.zeros((2 * LANES, LANES), own_ref.dtype)

    def where_of(step):
        if isinstance(step, int):
            return 0, step
        third, fourth = counts[0], counts[0] + counts[2]
        group = (step >= third).astype(jnp.int32) + (step >= fourth).astype(jnp.int32)
        start = jnp.where(step >= fourth, fourth, jnp.where(step >= third, third, 0))
        return group, step - start

    def push(step):
        group, at = where_of(step)
        for unit in range(2):
            parts = []
            for k in range(CHUNK):
                token, place = k // 2, (k + k // 2) % 2 * quarter
                slot = at * CHUNK + unit * CHUNK // 2 + token
                if not isinstance(step, int):
                    short = at * 2 * CHUNK + unit * CHUNK + k
                    slot = jnp.minimum(jnp.where(group == 0, slot, short), slots - 1)
                    place = jnp.where(group == 0, place, (group + 1) * quarter)
                    place = pl.multiple_of(place, quarter)
                lanes = pl.ds(place, quarter)
                parts += [own_ref[slot, lanes, :], sib_ref[slot, lanes, :]]
            tile = jnp.concatenate([jnp.concatenate(parts, axis=0), zeros], axis=1)
            pltpu.matmul_push_rhs(tile, 0, unit, transpose=True)

    def stream(part, load):
        rows = read_rows(part)
        rows = jnp.concatenate([rows, jnp.zeros_like(rows)], axis=1)
        for unit in range(2):
            pltpu.matmul_acc_lhs(units[part][unit], rows, 0 if load else None)

    def pop(part, step):
        group, at = where_of(step)
        best = jnp.maximum(pltpu.matmul_pop(units[part][0]), pltpu.matmul_pop(units[part][1]))
        if isinstance(step, int):
            acc[part][group] = best if at == 0 else jnp.maximum(acc[part][group], best)
        else:
            acc[part][group] = jnp.maximum(jnp.where(at == 0, LOWEST, acc[part][group]), best)

    push(0)
    stream(0, True)
    push(1)
    pop(0, 0)
    stream(1, False)
    pop(1, 0)
    counts = read_counts()
    last = counts[0] + counts[2] + counts[3] - 1
    stream(0, True)
    push(jnp.minimum(last, 2))
    stream(1, False)
    pop(0, 1)

    def body(step, _):
        stream(0, True)
        pop(1, step - 1)
        push(step + 1)
        stream(1, False)
        pop(0, step)
        return 0

    def finish(part):
        fresh = [pltpu.matmul_pop(unit) for unit in units[part]]
        for start in range(0, half, ROWS):
            rows = slice(start, start + ROWS)
            found = [acc[part][g, rows] for g in range(GROUPS)]
            found[-1] = jnp.maximum(found[-1], jnp.maximum(fresh[0][rows], fresh[1][rows]))
            long, third, fourth = [jnp.maximum(x[:, :LANES], x[:, LANES:]) for x in found]
            lane = lax.broadcasted_iota(jnp.int32, long.shape, 1)
            low = lane < 2 * width
            even = lane // width % 2 == 0
            short = jnp.maximum(
                jnp.where(low, third, fourth),
                pltpu.roll(jnp.where(low, fourth, third), 2 * width, 1),
            )
            best = jnp.maximum(
                jnp.where(even, short, long),
                pltpu.roll(jnp.where(even, long, short), LANES - width, 1),
            )
            partial = best.reshape(ROWS // TOKENS, TOKENS // 8, 8, LANES).sum(axis=1)
            spot = start * 8 // TOKENS
            sums[part, spot : spot + ROWS * 8 // TOKENS] = partial.reshape(-1, LANES)
        total = sums[part, pl.ds(0, half // TOKENS, stride=8), :]
        for k in range(1, 8):
            total = total + sums[part, pl.ds(k, half // TOKENS, stride=8), :]
        write(part, total)

    lax.fori_loop(2, last, body, 0)
    stream(0, True)
    pop(1, last - 1)
    stream(1, False)
    finish(0)
    finish(1)


def score_kernel(first, earlier, counts_ref, *refs):
    if earlier:
        ids_ref, *refs = refs
    own_ref, sib_ref, blocks_ref, *refs = refs
    pieces, refs = refs[:earlier], refs[earlier:]
    out_ref, acc_0, acc_1, sums, scores, counts_here, ids_here, arrived = refs
    load_counts = pltpu.make_async_copy(counts_ref, counts_here, arrived.at[0])
    load_counts.start()
    if earlier:
        load_ids = pltpu.make_async_copy(ids_ref, ids_here, arrived.at[1])
        load_ids.start()
    blocks, rows, dim = blocks_ref.shape
    step = min(blocks - first, BLOCKS)
    local = rows // TOKENS
    half = step * rows // 2
    planes, store, _ = own_ref.shape
    quarter = store // 4
    flat_ref = blocks_ref.reshape(blocks * rows, dim)
    at = sum(piece.shape[0] for piece in pieces)
    waited, placed = [], []

    def receive():
        if placed:
            return
        placed.append(load_ids.wait())
        spot = 0
        for piece in pieces:
            for block in range(piece.shape[0]):
                out_ref[ids_here[spot]] = piece[block]
                spot += 1

    def read_counts():
        if not waited:
            waited.append(load_counts.wait())
        return [counts_here[g] for g in range(4)]

    lane = lax.broadcasted_iota(jnp.int32, (16, LANES), 1)
    position = jnp.where(
        lane < store,
        own_ref[planes - 1, :16].astype(jnp.float32),
        sib_ref[planes - 1, :16].astype(jnp.float32) + quarter,
    ).astype(jnp.int32)[:1]

    def run(*units):
        def chunk(start):
            def read_rows(part):
                return flat_ref[pl.ds((first + start) * rows + part * half, half)]

            def write(part, total):
                count = half // TOKENS
                index = jnp.broadcast_to(position, (count, LANES))
                scores[part * count : (part + 1) * count] = jnp.take_along_axis(
                    total, index, axis=1
                )

            score_block(
                own_ref, sib_ref, read_rows, (acc_0, acc_1), sums,
                ((units[0], units[1]), (units[2], units[3])), read_counts, write,
            )
            if earlier:
                receive()
            for block in range(step):
                spot = ids_here[at + start + block] if earlier else start + block
                out_ref[spot] = scores[block * local : (block + 1) * local]

        if blocks - first == step:
            chunk(0)
        else:
            read_counts()
            if earlier:
                receive()
            pl.loop(0, blocks - first, step=step)(chunk)

    pl.run_scoped(run, *[pltpu.ACC(unit)((half, 2 * LANES), jnp.float32) for unit in (0, 1, 0, 1)])


def score(counts, own, sib, blocks, first=0, ids=None, earlier=()):
    count = blocks.shape[0] - first
    step = min(count, BLOCKS)
    half = step * blocks.shape[1] // 2
    local = blocks.shape[1] // TOKENS
    scalars = [counts] if ids is None else [counts, ids]
    operands = [own, sib, blocks, *earlier]
    total = count + sum(piece.shape[0] for piece in earlier)
    held = sum(x.size * x.dtype.itemsize for x in operands) + total * local * LANES * 4
    held += 2 * GROUPS * half * 2 * LANES * 4
    return pl.pallas_call(
        functools.partial(score_kernel, first, len(earlier)),
        out_shape=jax.ShapeDtypeStruct((total, local, 2 * own.shape[1]), jnp.float32),
        in_specs=[pl.BlockSpec(memory_space=pl.ANY)] * len(scalars) + [VMEM] * len(operands),
        out_specs=VMEM,
        scratch_shapes=[
            pltpu.VMEM((GROUPS, half, 2 * LANES), jnp.float32),
            pltpu.VMEM((GROUPS, half, 2 * LANES), jnp.float32),
            pltpu.VMEM((2, half * 8 // TOKENS, LANES), jnp.float32),
            pltpu.VMEM((step * local, LANES), jnp.float32),
            pltpu.SMEM(counts.shape, jnp.int32),
            pltpu.SMEM((total,), jnp.int32),
            pltpu.SemaphoreType.DMA((2,)),
        ],
        compiler_params=pltpu.CompilerParams(vmem_limit_bytes=held + (1 << 20)),
        cost_estimate=pl.CostEstimate(
            flops=8 * count * blocks[0].size * own.shape[0] * own.shape[1],
            bytes_accessed=4 * own.size,
            transcendentals=0,
        ),
        name="score",
    )(*scalars, *operands)


def pick_kernel(core_ref, table_ref, shard_ref, local_ref, out_ref):
    chips, rows, width = table_ref.shape
    store = width // 2
    for half in range(shard_ref.shape[1] // LANES):
        lanes = slice(half * LANES, half * LANES + LANES)
        shard = shard_ref[:, lanes]
        chip = chips - 1 - shard // 2
        lane = ((shard % 2) ^ core_ref[0]) * store + local_ref[:, lanes]
        total = jnp.zeros(lane.shape, jnp.float32)
        for k in range(chips):
            found = jnp.take_along_axis(table_ref[k], lane, axis=1)
            total = jnp.where(chip == k, found, total)
        out_ref[:, lanes] = total


def body(queries, cand_shard, cand_local, passages, lengths):
    me = lax.axis_index("psg").astype(jnp.int32)
    core = lax.axis_index("qry").reshape(1).astype(jnp.int32)
    chips = lax.axis_size("psg")
    local, qlen, dim = queries.shape

    def swap(a, bits):
        return lax.ppermute(a, "psg", [(i, i ^ bits) for i in range(chips)])

    own = prep(passages, lengths)
    rows = queries.reshape(1, local * qlen, dim)
    if chips == 16:
        others = [swap(rows, z) for z in (4, 8, 12)]
        own, *others = lax.optimization_barrier((own, *others))
        column = jnp.concatenate([rows] + others, axis=0)
    else:
        column, bit = rows, 4
        while bit < chips:
            column = jnp.concatenate([column, swap(column, bit)], axis=0)
            bit *= 2
    sib = lax.ppermute(own, "qry", [(0, 1), (1, 0)])
    counts = chunk_counts(own, sib)
    ids = (jnp.arange(0, chips, 4)[None, :] ^ jnp.arange(4)[:, None]).astype(jnp.int32) ^ me
    beside = [column] + [swap(column, k) for k in (1, 2, 3)]
    pieces = [score(counts, own, sib, column)]
    pieces += [score(counts, own, sib, beside[k]) for k in (1, 2)]
    ids = chips - 1 - ids.reshape(-1)
    table = score(counts, own, sib, beside[3], ids=ids, earlier=pieces)
    returned = lax.all_to_all(
        table, "psg", split_axis=0, concat_axis=0, tiled=True,
        axis_index_groups=[list(reversed(range(chips)))],
    )
    return pl.pallas_call(
        pick_kernel,
        out_shape=jax.ShapeDtypeStruct(cand_local.shape, jnp.float32),
        in_specs=[SMEM, VMEM, VMEM, VMEM],
        out_specs=VMEM,
        compiler_params=pltpu.CompilerParams(vmem_limit_bytes=4 << 20),
        name="pick",
    )(core, returned, cand_shard[:, :, 0], cand_local)


def solution(mesh):
    in_specs = (
        P(("psg", "qry"), None, None),
        P(("psg", "qry"), None, None),
        P(("psg", "qry"), None),
        P(("psg", "qry"), None, None),
        P(("psg", "qry")),
    )
    out_specs = P(("psg", "qry"), None)
    return jax.shard_map(body, mesh=mesh, in_specs=in_specs, out_specs=out_specs, check_vma=False)
```

```python
import functools

import jax
import jax.numpy as jnp
from jax import lax
from jax.experimental import pallas as pl
from jax.experimental.pallas import tpu as pltpu
from jax.sharding import PartitionSpec as P

VMEM = pl.BlockSpec(memory_space=pltpu.VMEM)
SMEM = pl.BlockSpec(memory_space=pltpu.SMEM)
TOKENS = 32
BLOCKS = 4
GROUPS = 3
CHUNK = 8
LANES = 128
ROWS = 128
LOWEST = -1e30


def prep_kernel(counts_ref, store_ref, out_ref, lengths_ref, passages_ref, arrived):
    load_lengths = pltpu.make_async_copy(counts_ref, lengths_ref, arrived.at[0])
    load_store = pltpu.make_async_copy(store_ref, passages_ref, arrived.at[1])
    load_lengths.start()
    load_store.start()
    load_lengths.wait()
    slots, store, dim = passages_ref.shape
    quarter = store // 4
    shape = (store, 2 * store)
    lengths = lengths_ref[...]
    along = jnp.broadcast_to(jnp.concatenate([lengths, lengths], axis=1), shape)
    row = lax.broadcasted_iota(jnp.int32, shape, 0)
    lane = lax.broadcasted_iota(jnp.int32, shape, 1)
    lane = jnp.where(lane >= store, lane - store, lane)
    down = jnp.sum(jnp.where(lane == row, along, 0), axis=1, keepdims=True) // 2
    longer = (down > along) | ((down == along) & (row < lane))
    rank = jnp.sum(longer.astype(jnp.int32), axis=0, keepdims=True)
    sorted_lengths = jnp.sum(jnp.where(rank == row, along, 0), axis=1, keepdims=True) // 2

    square = (2 * store, 2 * store)
    row = lax.broadcasted_iota(jnp.int32, square, 0)
    lane = lax.broadcasted_iota(jnp.int32, square, 1)
    target = rank + jnp.where(lane >= store, store, 0)
    order = (target == row).astype(jnp.float32).astype(passages_ref.dtype)

    load_store.wait()
    first = None
    for t in range(0, slots, 2):
        pair = passages_ref[t : t + 2].reshape(2 * store, dim)
        moved = jnp.dot(order, pair, preferred_element_type=jnp.float32).reshape(2, store, dim)
        first = moved[0] if first is None else first
        for k in range(2):
            out_ref[t + k] = jnp.where(t + k < sorted_lengths, moved[k], first).astype(out_ref.dtype)
    place = rank // quarter
    place = jnp.where(place == 0, 3, jnp.where(place == 1, 1, jnp.where(place == 2, 0, 2)))
    place = place * 2 * quarter + rank % quarter
    for k, value in enumerate((sorted_lengths, place)):
        value = jnp.broadcast_to(value, (store, dim)).astype(jnp.float32)
        out_ref[slots + k] = value.astype(out_ref.dtype)


def prep(passages, lengths):
    store, slots, dim = passages.shape
    return pl.pallas_call(
        prep_kernel,
        out_shape=jax.ShapeDtypeStruct((slots + 2, store, dim), passages.dtype),
        in_specs=[pl.BlockSpec(memory_space=pl.ANY)] * 2,
        out_specs=VMEM,
        scratch_shapes=[
            pltpu.VMEM((1, store), jnp.int32),
            pltpu.VMEM((slots, store, dim), passages.dtype),
            pltpu.SemaphoreType.DMA((2,)),
        ],
        compiler_params=pltpu.CompilerParams(vmem_limit_bytes=4 << 20),
        cost_estimate=pl.CostEstimate(
            flops=64 * passages.size * store, bytes_accessed=4 * passages.size, transcendentals=0
        ),
        name="prep",
    )(
        pltpu.with_memory_space_constraint(lengths.reshape(1, store), pltpu.HBM),
        pltpu.with_memory_space_constraint(passages.transpose(1, 0, 2), pltpu.HBM),
    )


def chunk_counts(own, sib):
    quarter = own.shape[1] // 4
    longest = [plane[-2, ::quarter, 0].astype(jnp.int32) for plane in (own, sib)]
    at_once = CHUNK * (1 + jnp.arange(4, dtype=jnp.int32) // 2)
    counts = (jnp.maximum(*longest) + at_once - 1) // at_once
    return jnp.maximum(counts, 2)


def score_block(own_ref, sib_ref, read_rows, acc, sums, units, read_counts, write):
    half = acc[0].shape[1]
    slots = own_ref.shape[0] - 2
    quarter = own_ref.shape[1] // 4
    width = 2 * quarter
    zeros = jnp.zeros((2 * LANES, LANES), own_ref.dtype)

    def where_of(step):
        if isinstance(step, int):
            return 0, step
        third, fourth = counts[0], counts[0] + counts[2]
        group = (step >= third).astype(jnp.int32) + (step >= fourth).astype(jnp.int32)
        start = jnp.where(step >= fourth, fourth, jnp.where(step >= third, third, 0))
        return group, step - start

    def push(step):
        group, at = where_of(step)
        for unit in range(2):
            parts = []
            for k in range(CHUNK):
                token, place = k // 2, (k + k // 2) % 2 * quarter
                slot = at * CHUNK + unit * CHUNK // 2 + token
                if not isinstance(step, int):
                    short = at * 2 * CHUNK + unit * CHUNK + k
                    slot = jnp.minimum(jnp.where(group == 0, slot, short), slots - 1)
                    place = jnp.where(group == 0, place, (group + 1) * quarter)
                    place = pl.multiple_of(place, quarter)
                lanes = pl.ds(place, quarter)
                parts += [own_ref[slot, lanes, :], sib_ref[slot, lanes, :]]
            tile = jnp.concatenate([jnp.concatenate(parts, axis=0), zeros], axis=1)
            pltpu.matmul_push_rhs(tile, 0, unit, transpose=True)

    def stream(part, load):
        rows = read_rows(part)
        rows = jnp.concatenate([rows, jnp.zeros_like(rows)], axis=1)
        for unit in range(2):
            pltpu.matmul_acc_lhs(units[part][unit], rows, 0 if load else None)

    def pop(part, step):
        group, at = where_of(step)
        best = jnp.maximum(pltpu.matmul_pop(units[part][0]), pltpu.matmul_pop(units[part][1]))
        if isinstance(step, int):
            acc[part][group] = best if at == 0 else jnp.maximum(acc[part][group], best)
        else:
            acc[part][group] = jnp.maximum(jnp.where(at == 0, LOWEST, acc[part][group]), best)

    push(0)
    stream(0, True)
    push(1)
    pop(0, 0)
    stream(1, False)
    pop(1, 0)
    counts = read_counts()
    last = counts[0] + counts[2] + counts[3] - 1
    stream(0, True)
    push(jnp.minimum(last, 2))
    stream(1, False)
    pop(0, 1)

    def body(step, _):
        stream(0, True)
        pop(1, step - 1)
        push(step + 1)
        stream(1, False)
        pop(0, step)
        return 0

    def finish(part):
        fresh = [pltpu.matmul_pop(unit) for unit in units[part]]
        for start in range(0, half, ROWS):
            rows = slice(start, start + ROWS)
            found = [acc[part][g, rows] for g in range(GROUPS)]
            found[-1] = jnp.maximum(found[-1], jnp.maximum(fresh[0][rows], fresh[1][rows]))
            long, third, fourth = [jnp.maximum(x[:, :LANES], x[:, LANES:]) for x in found]
            lane = lax.broadcasted_iota(jnp.int32, long.shape, 1)
            low = lane < 2 * width
            even = lane // width % 2 == 0
            short = jnp.maximum(
                jnp.where(low, third, fourth),
                pltpu.roll(jnp.where(low, fourth, third), 2 * width, 1),
            )
            best = jnp.maximum(
                jnp.where(even, short, long),
                pltpu.roll(jnp.where(even, long, short), LANES - width, 1),
            )
            partial = best.reshape(ROWS // TOKENS, TOKENS // 8, 8, LANES).sum(axis=1)
            spot = start * 8 // TOKENS
            sums[part, spot : spot + ROWS * 8 // TOKENS] = partial.reshape(-1, LANES)
        total = sums[part, pl.ds(0, half // TOKENS, stride=8), :]
        for k in range(1, 8):
            total = total + sums[part, pl.ds(k, half // TOKENS, stride=8), :]
        write(part, total)

    lax.fori_loop(2, last, body, 0)
    stream(0, True)
    pop(1, last - 1)
    stream(1, False)
    finish(0)
    finish(1)


def score_kernel(first, earlier, counts_ref, *refs):
    if earlier:
        ids_ref, *refs = refs
    own_ref, sib_ref, blocks_ref, *refs = refs
    pieces, refs = refs[:earlier], refs[earlier:]
    out_ref, acc_0, acc_1, sums, scores, counts_here, ids_here, arrived = refs
    load_counts = pltpu.make_async_copy(counts_ref, counts_here, arrived.at[0])
    load_counts.start()
    if earlier:
        load_ids = pltpu.make_async_copy(ids_ref, ids_here, arrived.at[1])
        load_ids.start()
    blocks, rows, dim = blocks_ref.shape
    step = min(blocks - first, BLOCKS)
    local = rows // TOKENS
    half = step * rows // 2
    planes, store, _ = own_ref.shape
    quarter = store // 4
    flat_ref = blocks_ref.reshape(blocks * rows, dim)
    at = sum(piece.shape[0] for piece in pieces)
    waited, placed = [], []

    def receive():
        if placed:
            return
        placed.append(load_ids.wait())
        spot = 0
        for piece in pieces:
            for block in range(piece.shape[0]):
                out_ref[ids_here[spot]] = piece[block]
                spot += 1

    def read_counts():
        if not waited:
            waited.append(load_counts.wait())
        return [counts_here[g] for g in range(4)]

    lane = lax.broadcasted_iota(jnp.int32, (16, LANES), 1)
    position = jnp.where(
        lane < store,
        own_ref[planes - 1, :16].astype(jnp.float32),
        sib_ref[planes - 1, :16].astype(jnp.float32) + quarter,
    ).astype(jnp.int32)[:1]

    def run(*units):
        def chunk(start):
            def read_rows(part):
                return flat_ref[pl.ds((first + start) * rows + part * half, half)]

            def write(part, total):
                count = half // TOKENS
                index = jnp.broadcast_to(position, (count, LANES))
                scores[part * count : (part + 1) * count] = jnp.take_along_axis(
                    total, index, axis=1
                )

            score_block(
                own_ref, sib_ref, read_rows, (acc_0, acc_1), sums,
                ((units[0], units[1]), (units[2], units[3])), read_counts, write,
            )
            if earlier:
                receive()
            for block in range(step):
                spot = ids_here[at + start + block] if earlier else start + block
                out_ref[spot] = scores[block * local : (block + 1) * local]

        if blocks - first == step:
            chunk(0)
        else:
            read_counts()
            if earlier:
                receive()
            pl.loop(0, blocks - first, step=step)(chunk)

    pl.run_scoped(run, *[pltpu.ACC(unit)((half, 2 * LANES), jnp.float32) for unit in (0, 1, 0, 1)])


def score(counts, own, sib, blocks, first=0, ids=None, earlier=()):
    count = blocks.shape[0] - first
    step = min(count, BLOCKS)
    half = step * blocks.shape[1] // 2
    local = blocks.shape[1] // TOKENS
    scalars = [counts] if ids is None else [counts, ids]
    operands = [own, sib, blocks, *earlier]
    total = count + sum(piece.shape[0] for piece in earlier)
    held = sum(x.size * x.dtype.itemsize for x in operands) + total * local * LANES * 4
    held += 2 * GROUPS * half * 2 * LANES * 4
    return pl.pallas_call(
        functools.partial(score_kernel, first, len(earlier)),
        out_shape=jax.ShapeDtypeStruct((total, local, 2 * own.shape[1]), jnp.float32),
        in_specs=[pl.BlockSpec(memory_space=pl.ANY)] * len(scalars) + [VMEM] * len(operands),
        out_specs=VMEM,
        scratch_shapes=[
            pltpu.VMEM((GROUPS, half, 2 * LANES), jnp.float32),
            pltpu.VMEM((GROUPS, half, 2 * LANES), jnp.float32),
            pltpu.VMEM((2, half * 8 // TOKENS, LANES), jnp.float32),
            pltpu.VMEM((step * local, LANES), jnp.float32),
            pltpu.SMEM(counts.shape, jnp.int32),
            pltpu.SMEM((total,), jnp.int32),
            pltpu.SemaphoreType.DMA((2,)),
        ],
        compiler_params=pltpu.CompilerParams(vmem_limit_bytes=held + (1 << 20)),
        cost_estimate=pl.CostEstimate(
            flops=8 * count * blocks[0].size * own.shape[0] * own.shape[1],
            bytes_accessed=4 * own.size,
            transcendentals=0,
        ),
        name="score",
    )(*scalars, *operands)


def pick_kernel(core_ref, table_ref, shard_ref, local_ref, out_ref):
    chips, rows, width = table_ref.shape
    store = width // 2
    for half in range(shard_ref.shape[1] // LANES):
        lanes = slice(half * LANES, half * LANES + LANES)
        shard = shard_ref[:, lanes]
        chip = chips - 1 - shard // 2
        lane = ((shard % 2) ^ core_ref[0]) * store + local_ref[:, lanes]
        total = jnp.zeros(lane.shape, jnp.float32)
        for k in range(chips):
            found = jnp.take_along_axis(table_ref[k], lane, axis=1)
            total = jnp.where(chip == k, found, total)
        out_ref[:, lanes] = total


def body(queries, cand_shard, cand_local, passages, lengths):
    me = lax.axis_index("psg").astype(jnp.int32)
    core = lax.axis_index("qry").reshape(1).astype(jnp.int32)
    chips = lax.axis_size("psg")
    local, qlen, dim = queries.shape

    def swap(a, bits):
        return lax.ppermute(a, "psg", [(i, i ^ bits) for i in range(chips)])

    own = prep(passages, lengths)
    rows = queries.reshape(1, local * qlen, dim)
    if chips == 16:
        others = [swap(rows, z) for z in (12, 4, 8)]
        own, *others = lax.optimization_barrier((own, *others))
        column = jnp.concatenate([rows] + others, axis=0)
    else:
        column, bit = rows, 4
        while bit < chips:
            column = jnp.concatenate([column, swap(column, bit)], axis=0)
            bit *= 2
    sib = lax.ppermute(own, "qry", [(0, 1), (1, 0)])
    counts = chunk_counts(own, sib)
    near = jnp.array([0, 12, 4, 8]) if chips == 16 else jnp.arange(0, chips, 4)
    ids = (near[None, :] ^ jnp.arange(4)[:, None]).astype(jnp.int32) ^ me
    beside = [column] + [swap(column, k) for k in (1, 2, 3)]
    pieces = [score(counts, own, sib, column)]
    pieces += [score(counts, own, sib, beside[k]) for k in (1, 2)]
    ids = chips - 1 - ids.reshape(-1)
    table = score(counts, own, sib, beside[3], ids=ids, earlier=pieces)
    returned = lax.all_to_all(
        table, "psg", split_axis=0, concat_axis=0, tiled=True,
        axis_index_groups=[list(reversed(range(chips)))],
    )
    return pl.pallas_call(
        pick_kernel,
        out_shape=jax.ShapeDtypeStruct(cand_local.shape, jnp.float32),
        in_specs=[SMEM, VMEM, VMEM, VMEM],
        out_specs=VMEM,
        compiler_params=pltpu.CompilerParams(vmem_limit_bytes=4 << 20),
        name="pick",
    )(core, returned, cand_shard[:, :, 0], cand_local)


def solution(mesh):
    in_specs = (
        P(("psg", "qry"), None, None),
        P(("psg", "qry"), None, None),
        P(("psg", "qry"), None),
        P(("psg", "qry"), None, None),
        P(("psg", "qry")),
    )
    out_specs = P(("psg", "qry"), None)
    return jax.shard_map(body, mesh=mesh, in_specs=in_specs, out_specs=out_specs, check_vma=False)
```

```python
import functools

import jax
import jax.numpy as jnp
from jax import lax
from jax.experimental import pallas as pl
from jax.experimental.pallas import tpu as pltpu
from jax.sharding import PartitionSpec as P

VMEM = pl.BlockSpec(memory_space=pltpu.VMEM)
SMEM = pl.BlockSpec(memory_space=pltpu.SMEM)
TOKENS = 32
BLOCKS = 4
GROUPS = 3
CHUNK = 8
LANES = 128
ROWS = 128
LOWEST = -1e30


def prep_kernel(counts_ref, store_ref, out_ref, lengths_ref, passages_ref, arrived):
    load_lengths = pltpu.make_async_copy(counts_ref, lengths_ref, arrived.at[0])
    load_store = pltpu.make_async_copy(store_ref, passages_ref, arrived.at[1])
    load_lengths.start()
    load_store.start()
    load_lengths.wait()
    slots, store, dim = passages_ref.shape
    quarter = store // 4
    shape = (store, 2 * store)
    lengths = lengths_ref[...]
    along = jnp.broadcast_to(jnp.concatenate([lengths, lengths], axis=1), shape)
    row = lax.broadcasted_iota(jnp.int32, shape, 0)
    lane = lax.broadcasted_iota(jnp.int32, shape, 1)
    lane = jnp.where(lane >= store, lane - store, lane)
    down = jnp.sum(jnp.where(lane == row, along, 0), axis=1, keepdims=True) // 2
    longer = (down > along) | ((down == along) & (row < lane))
    rank = jnp.sum(longer.astype(jnp.int32), axis=0, keepdims=True)
    sorted_lengths = jnp.sum(jnp.where(rank == row, along, 0), axis=1, keepdims=True) // 2

    square = (2 * store, 2 * store)
    row = lax.broadcasted_iota(jnp.int32, square, 0)
    lane = lax.broadcasted_iota(jnp.int32, square, 1)
    target = rank + jnp.where(lane >= store, store, 0)
    order = (target == row).astype(jnp.float32).astype(passages_ref.dtype)

    load_store.wait()
    first = None
    for t in range(0, slots, 2):
        pair = passages_ref[t : t + 2].reshape(2 * store, dim)
        moved = jnp.dot(order, pair, preferred_element_type=jnp.float32).reshape(2, store, dim)
        first = moved[0] if first is None else first
        for k in range(2):
            out_ref[t + k] = jnp.where(t + k < sorted_lengths, moved[k], first).astype(out_ref.dtype)
    place = rank // quarter
    place = jnp.where(place == 0, 3, jnp.where(place == 1, 1, jnp.where(place == 2, 0, 2)))
    place = place * 2 * quarter + rank % quarter
    for k, value in enumerate((sorted_lengths, place)):
        value = jnp.broadcast_to(value, (store, dim)).astype(jnp.float32)
        out_ref[slots + k] = value.astype(out_ref.dtype)


def prep(passages, lengths):
    store, slots, dim = passages.shape
    return pl.pallas_call(
        prep_kernel,
        out_shape=jax.ShapeDtypeStruct((slots + 2, store, dim), passages.dtype),
        in_specs=[pl.BlockSpec(memory_space=pl.ANY)] * 2,
        out_specs=VMEM,
        scratch_shapes=[
            pltpu.VMEM((1, store), jnp.int32),
            pltpu.VMEM((slots, store, dim), passages.dtype),
            pltpu.SemaphoreType.DMA((2,)),
        ],
        compiler_params=pltpu.CompilerParams(vmem_limit_bytes=4 << 20),
        cost_estimate=pl.CostEstimate(
            flops=64 * passages.size * store, bytes_accessed=4 * passages.size, transcendentals=0
        ),
        name="prep",
    )(
        pltpu.with_memory_space_constraint(lengths.reshape(1, store), pltpu.HBM),
        pltpu.with_memory_space_constraint(passages.transpose(1, 0, 2), pltpu.HBM),
    )


def chunk_counts(own, sib):
    quarter = own.shape[1] // 4
    longest = [plane[-2, ::quarter, 0].astype(jnp.int32) for plane in (own, sib)]
    halves = 2 - (jnp.arange(4, dtype=jnp.int32) >> 1)
    counts = (jnp.maximum(*longest) * halves + 2 * CHUNK - 1) // (2 * CHUNK)
    return jnp.maximum(counts, 2)


def score_block(own_ref, sib_ref, read_rows, acc, sums, units, read_counts, write):
    half = acc[0].shape[1]
    slots = own_ref.shape[0] - 2
    quarter = own_ref.shape[1] // 4
    width = 2 * quarter
    zeros = jnp.zeros((2 * LANES, LANES), own_ref.dtype)

    def where_of(step):
        if isinstance(step, int):
            return 0, step
        third, fourth = counts[0], counts[0] + counts[2]
        group = (step >= third).astype(jnp.int32) + (step >= fourth).astype(jnp.int32)
        start = jnp.where(step >= fourth, fourth, jnp.where(step >= third, third, 0))
        return group, step - start

    def push(step):
        group, at = where_of(step)
        for unit in range(2):
            parts = []
            for k in range(CHUNK):
                token, place = k // 2, (k + k // 2) % 2 * quarter
                slot = at * CHUNK + unit * CHUNK // 2 + token
                if not isinstance(step, int):
                    short = at * 2 * CHUNK + unit * CHUNK + k
                    slot = jnp.minimum(jnp.where(group == 0, slot, short), slots - 1)
                    place = jnp.where(group == 0, place, (group + 1) * quarter)
                    place = pl.multiple_of(place, quarter)
                lanes = pl.ds(place, quarter)
                parts += [own_ref[slot, lanes, :], sib_ref[slot, lanes, :]]
            tile = jnp.concatenate([jnp.concatenate(parts, axis=0), zeros], axis=1)
            pltpu.matmul_push_rhs(tile, 0, unit, transpose=True)

    def stream(part, load):
        rows = read_rows(part)
        rows = jnp.concatenate([rows, jnp.zeros_like(rows)], axis=1)
        for unit in range(2):
            pltpu.matmul_acc_lhs(units[part][unit], rows, 0 if load else None)

    def pop(part, step):
        group, at = where_of(step)
        best = jnp.maximum(pltpu.matmul_pop(units[part][0]), pltpu.matmul_pop(units[part][1]))
        if isinstance(step, int):
            acc[part][group] = best if at == 0 else jnp.maximum(acc[part][group], best)
        else:
            acc[part][group] = jnp.maximum(jnp.where(at == 0, LOWEST, acc[part][group]), best)

    push(0)
    stream(0, True)
    push(1)
    pop(0, 0)
    stream(1, False)
    pop(1, 0)
    counts = read_counts()
    last = counts[0] + counts[2] + counts[3] - 1
    stream(0, True)
    push(jnp.minimum(last, 2))
    stream(1, False)
    pop(0, 1)

    def body(step, _):
        stream(0, True)
        pop(1, step - 1)
        push(step + 1)
        stream(1, False)
        pop(0, step)
        return 0

    def finish(part):
        fresh = [pltpu.matmul_pop(unit) for unit in units[part]]
        for start in range(0, half, ROWS):
            rows = slice(start, start + ROWS)
            found = [acc[part][g, rows] for g in range(GROUPS)]
            found[-1] = jnp.maximum(found[-1], jnp.maximum(fresh[0][rows], fresh[1][rows]))
            long, third, fourth = [jnp.maximum(x[:, :LANES], x[:, LANES:]) for x in found]
            lane = lax.broadcasted_iota(jnp.int32, long.shape, 1)
            low = lane < 2 * width
            even = lane // width % 2 == 0
            short = jnp.maximum(
                jnp.where(low, third, fourth),
                pltpu.roll(jnp.where(low, fourth, third), 2 * width, 1),
            )
            best = jnp.maximum(
                jnp.where(even, short, long),
                pltpu.roll(jnp.where(even, long, short), LANES - width, 1),
            )
            partial = best.reshape(ROWS // TOKENS, TOKENS // 8, 8, LANES).sum(axis=1)
            spot = start * 8 // TOKENS
            sums[part, spot : spot + ROWS * 8 // TOKENS] = partial.reshape(-1, LANES)
        total = sums[part, pl.ds(0, half // TOKENS, stride=8), :]
        for k in range(1, 8):
            total = total + sums[part, pl.ds(k, half // TOKENS, stride=8), :]
        write(part, total)

    lax.fori_loop(2, last, body, 0)
    stream(0, True)
    pop(1, last - 1)
    stream(1, False)
    finish(0)
    finish(1)


def score_kernel(first, earlier, counts_ref, *refs):
    if earlier:
        ids_ref, *refs = refs
    own_ref, sib_ref, blocks_ref, *refs = refs
    pieces, refs = refs[:earlier], refs[earlier:]
    out_ref, acc_0, acc_1, sums, scores, counts_here, ids_here, arrived = refs
    load_counts = pltpu.make_async_copy(counts_ref, counts_here, arrived.at[0])
    load_counts.start()
    if earlier:
        load_ids = pltpu.make_async_copy(ids_ref, ids_here, arrived.at[1])
        load_ids.start()
    blocks, rows, dim = blocks_ref.shape
    step = min(blocks - first, BLOCKS)
    local = rows // TOKENS
    half = step * rows // 2
    planes, store, _ = own_ref.shape
    quarter = store // 4
    flat_ref = blocks_ref.reshape(blocks * rows, dim)
    at = sum(piece.shape[0] for piece in pieces)
    waited, placed = [], []

    def receive():
        if placed:
            return
        placed.append(load_ids.wait())
        spot = 0
        for piece in pieces:
            for block in range(piece.shape[0]):
                out_ref[ids_here[spot]] = piece[block]
                spot += 1

    def read_counts():
        if not waited:
            waited.append(load_counts.wait())
        return [counts_here[g] for g in range(4)]

    lane = lax.broadcasted_iota(jnp.int32, (16, LANES), 1)
    position = jnp.where(
        lane < store,
        own_ref[planes - 1, :16].astype(jnp.float32),
        sib_ref[planes - 1, :16].astype(jnp.float32) + quarter,
    ).astype(jnp.int32)[:1]

    def run(*units):
        def chunk(start):
            def read_rows(part):
                return flat_ref[pl.ds((first + start) * rows + part * half, half)]

            def write(part, total):
                count = half // TOKENS
                index = jnp.broadcast_to(position, (count, LANES))
                scores[part * count : (part + 1) * count] = jnp.take_along_axis(
                    total, index, axis=1
                )

            score_block(
                own_ref, sib_ref, read_rows, (acc_0, acc_1), sums,
                ((units[0], units[1]), (units[2], units[3])), read_counts, write,
            )
            if earlier:
                receive()
            for block in range(step):
                spot = ids_here[at + start + block] if earlier else start + block
                out_ref[spot] = scores[block * local : (block + 1) * local]

        if blocks - first == step:
            chunk(0)
        else:
            read_counts()
            if earlier:
                receive()
            pl.loop(0, blocks - first, step=step)(chunk)

    pl.run_scoped(run, *[pltpu.ACC(unit)((half, 2 * LANES), jnp.float32) for unit in (0, 1, 0, 1)])


def score(counts, own, sib, blocks, first=0, ids=None, earlier=()):
    count = blocks.shape[0] - first
    step = min(count, BLOCKS)
    half = step * blocks.shape[1] // 2
    local = blocks.shape[1] // TOKENS
    scalars = [counts] if ids is None else [counts, ids]
    operands = [own, sib, blocks, *earlier]
    total = count + sum(piece.shape[0] for piece in earlier)
    held = sum(x.size * x.dtype.itemsize for x in operands) + total * local * LANES * 4
    held += 2 * GROUPS * half * 2 * LANES * 4
    return pl.pallas_call(
        functools.partial(score_kernel, first, len(earlier)),
        out_shape=jax.ShapeDtypeStruct((total, local, 2 * own.shape[1]), jnp.float32),
        in_specs=[pl.BlockSpec(memory_space=pl.ANY)] * len(scalars) + [VMEM] * len(operands),
        out_specs=VMEM,
        scratch_shapes=[
            pltpu.VMEM((GROUPS, half, 2 * LANES), jnp.float32),
            pltpu.VMEM((GROUPS, half, 2 * LANES), jnp.float32),
            pltpu.VMEM((2, half * 8 // TOKENS, LANES), jnp.float32),
            pltpu.VMEM((step * local, LANES), jnp.float32),
            pltpu.SMEM(counts.shape, jnp.int32),
            pltpu.SMEM((total,), jnp.int32),
            pltpu.SemaphoreType.DMA((2,)),
        ],
        compiler_params=pltpu.CompilerParams(vmem_limit_bytes=held + (1 << 20)),
        cost_estimate=pl.CostEstimate(
            flops=8 * count * blocks[0].size * own.shape[0] * own.shape[1],
            bytes_accessed=4 * own.size,
            transcendentals=0,
        ),
        name="score",
    )(*scalars, *operands)


def pick_kernel(core_ref, table_ref, shard_ref, local_ref, out_ref):
    chips, rows, width = table_ref.shape
    store = width // 2
    for half in range(shard_ref.shape[1] // LANES):
        lanes = slice(half * LANES, half * LANES + LANES)
        shard = shard_ref[:, lanes]
        chip = chips - 1 - shard // 2
        lane = ((shard % 2) ^ core_ref[0]) * store + local_ref[:, lanes]
        total = jnp.zeros(lane.shape, jnp.float32)
        for k in range(chips):
            found = jnp.take_along_axis(table_ref[k], lane, axis=1)
            total = jnp.where(chip == k, found, total)
        out_ref[:, lanes] = total


def body(queries, cand_shard, cand_local, passages, lengths):
    me = lax.axis_index("psg").astype(jnp.int32)
    core = lax.axis_index("qry").reshape(1).astype(jnp.int32)
    chips = lax.axis_size("psg")
    local, qlen, dim = queries.shape

    def swap(a, bits):
        return lax.ppermute(a, "psg", [(i, i ^ bits) for i in range(chips)])

    own = prep(passages, lengths)
    rows = queries.reshape(1, local * qlen, dim)
    if chips == 16:
        others = [swap(rows, z) for z in (12, 4, 8)]
        own, *others = lax.optimization_barrier((own, *others))
        column = jnp.concatenate([rows] + others, axis=0)
    else:
        column, bit = rows, 4
        while bit < chips:
            column = jnp.concatenate([column, swap(column, bit)], axis=0)
            bit *= 2
    sib = lax.ppermute(own, "qry", [(0, 1), (1, 0)])
    counts = chunk_counts(own, sib)
    near = jnp.array([0, 12, 4, 8]) if chips == 16 else jnp.arange(0, chips, 4)
    ids = (near[None, :] ^ jnp.arange(4)[:, None]).astype(jnp.int32) ^ me
    beside = [column] + [swap(column, k) for k in (1, 2, 3)]
    pieces = [score(counts, own, sib, column)]
    pieces += [score(counts, own, sib, beside[k]) for k in (1, 2)]
    ids = chips - 1 - ids.reshape(-1)
    table = score(counts, own, sib, beside[3], ids=ids, earlier=pieces)
    returned = lax.all_to_all(
        table, "psg", split_axis=0, concat_axis=0, tiled=True,
        axis_index_groups=[list(reversed(range(chips)))],
    )
    return pl.pallas_call(
        pick_kernel,
        out_shape=jax.ShapeDtypeStruct(cand_local.shape, jnp.float32),
        in_specs=[SMEM, VMEM, VMEM, VMEM],
        out_specs=VMEM,
        compiler_params=pltpu.CompilerParams(vmem_limit_bytes=4 << 20),
        name="pick",
    )(core, returned, cand_shard[:, :, 0], cand_local)


def solution(mesh):
    in_specs = (
        P(("psg", "qry"), None, None),
        P(("psg", "qry"), None, None),
        P(("psg", "qry"), None),
        P(("psg", "qry"), None, None),
        P(("psg", "qry")),
    )
    out_specs = P(("psg", "qry"), None)
    return jax.shard_map(body, mesh=mesh, in_specs=in_specs, out_specs=out_specs, check_vma=False)
```

```python
import functools

import jax
import jax.numpy as jnp
from jax import lax
from jax.experimental import pallas as pl
from jax.experimental.pallas import tpu as pltpu
from jax.sharding import PartitionSpec as P

VMEM = pl.BlockSpec(memory_space=pltpu.VMEM)
SMEM = pl.BlockSpec(memory_space=pltpu.SMEM)
TOKENS = 32
BLOCKS = 4
GROUPS = 3
CHUNK = 8
LANES = 128
ROWS = 128
LOWEST = -1e30


def prep_kernel(counts_ref, store_ref, out_ref, lengths_ref, passages_ref, arrived):
    load_lengths = pltpu.make_async_copy(counts_ref, lengths_ref, arrived.at[0])
    load_store = pltpu.make_async_copy(store_ref, passages_ref, arrived.at[1])
    load_lengths.start()
    load_store.start()
    load_lengths.wait()
    slots, store, dim = passages_ref.shape
    quarter = store // 4
    shape = (store, 2 * store)
    lengths = lengths_ref[...]
    along = jnp.broadcast_to(jnp.concatenate([lengths, lengths], axis=1), shape)
    row = lax.broadcasted_iota(jnp.int32, shape, 0)
    lane = lax.broadcasted_iota(jnp.int32, shape, 1)
    lane = jnp.where(lane >= store, lane - store, lane)
    down = jnp.sum(jnp.where(lane == row, along, 0), axis=1, keepdims=True) // 2
    longer = (down > along) | ((down == along) & (row < lane))
    rank = jnp.sum(longer.astype(jnp.int32), axis=0, keepdims=True)
    sorted_lengths = jnp.sum(jnp.where(rank == row, along, 0), axis=1, keepdims=True) // 2

    square = (2 * store, 2 * store)
    row = lax.broadcasted_iota(jnp.int32, square, 0)
    lane = lax.broadcasted_iota(jnp.int32, square, 1)
    target = rank + jnp.where(lane >= store, store, 0)
    order = (target == row).astype(jnp.float32).astype(passages_ref.dtype)

    load_store.wait()
    first = None
    for t in range(0, slots, 2):
        pair = passages_ref[t : t + 2].reshape(2 * store, dim)
        moved = jnp.dot(order, pair, preferred_element_type=jnp.float32).reshape(2, store, dim)
        first = moved[0] if first is None else first
        for k in range(2):
            out_ref[t + k] = jnp.where(t + k < sorted_lengths, moved[k], first).astype(out_ref.dtype)
    place = rank // quarter
    place = jnp.where(place == 0, 3, jnp.where(place == 1, 1, jnp.where(place == 2, 0, 2)))
    place = place * 2 * quarter + rank % quarter
    for k, value in enumerate((sorted_lengths, place)):
        value = jnp.broadcast_to(value, (store, dim)).astype(jnp.float32)
        out_ref[slots + k] = value.astype(out_ref.dtype)


def prep(passages, lengths):
    store, slots, dim = passages.shape
    return pl.pallas_call(
        prep_kernel,
        out_shape=jax.ShapeDtypeStruct((slots + 2, store, dim), passages.dtype),
        in_specs=[pl.BlockSpec(memory_space=pl.ANY)] * 2,
        out_specs=VMEM,
        scratch_shapes=[
            pltpu.VMEM((1, store), jnp.int32),
            pltpu.VMEM((slots, store, dim), passages.dtype),
            pltpu.SemaphoreType.DMA((2,)),
        ],
        compiler_params=pltpu.CompilerParams(vmem_limit_bytes=4 << 20),
        cost_estimate=pl.CostEstimate(
            flops=64 * passages.size * store, bytes_accessed=4 * passages.size, transcendentals=0
        ),
        name="prep",
    )(
        pltpu.with_memory_space_constraint(lengths.reshape(1, store), pltpu.HBM),
        pltpu.with_memory_space_constraint(passages.transpose(1, 0, 2), pltpu.HBM),
    )


def chunk_counts(own, sib):
    quarter = own.shape[1] // 4
    longest = [plane[-2, ::quarter, 0].astype(jnp.int32) for plane in (own, sib)]
    halves = 2 - (jnp.arange(4, dtype=jnp.int32) >> 1)
    counts = (jnp.maximum(*longest) * halves + 2 * CHUNK - 1) // (2 * CHUNK)
    return jnp.maximum(counts, 2)


def score_block(own_ref, sib_ref, read_rows, acc, sums, units, read_counts, write):
    half = acc[0].shape[1]
    slots = own_ref.shape[0] - 2
    quarter = own_ref.shape[1] // 4
    width = 2 * quarter
    zeros = jnp.zeros((2 * LANES, LANES), own_ref.dtype)

    def where_of(step):
        if isinstance(step, int):
            return 0, step
        third, fourth = counts[0], counts[0] + counts[2]
        group = (step >= third).astype(jnp.int32) + (step >= fourth).astype(jnp.int32)
        start = jnp.where(step >= fourth, fourth, jnp.where(step >= third, third, 0))
        return group, step - start

    def push(step):
        group, at = where_of(step)
        for unit in range(2):
            parts = []
            for k in range(CHUNK):
                token, place = k // 2, (k + k // 2) % 2 * quarter
                slot = at * CHUNK + unit * CHUNK // 2 + token
                if not isinstance(step, int):
                    short = at * 2 * CHUNK + unit * CHUNK + k
                    slot = jnp.minimum(jnp.where(group == 0, slot, short), slots - 1)
                    place = jnp.where(group == 0, place, (group + 1) * quarter)
                    place = pl.multiple_of(place, quarter)
                lanes = pl.ds(place, quarter)
                parts += [own_ref[slot, lanes, :], sib_ref[slot, lanes, :]]
            tile = jnp.concatenate([jnp.concatenate(parts, axis=0), zeros], axis=1)
            pltpu.matmul_push_rhs(tile, 0, unit, transpose=True)

    def stream(part, load):
        rows = read_rows(part)
        rows = jnp.concatenate([rows, jnp.zeros_like(rows)], axis=1)
        for unit in range(2):
            pltpu.matmul_acc_lhs(units[part][unit], rows, 0 if load else None)

    def pop(part, step):
        group, at = where_of(step)
        best = jnp.maximum(pltpu.matmul_pop(units[part][0]), pltpu.matmul_pop(units[part][1]))
        if isinstance(step, int):
            acc[part][group] = best if at == 0 else jnp.maximum(acc[part][group], best)
        else:
            acc[part][group] = jnp.maximum(jnp.where(at == 0, LOWEST, acc[part][group]), best)

    push(0)
    stream(0, True)
    push(1)
    pop(0, 0)
    stream(1, False)
    pop(1, 0)
    counts = read_counts()
    last = counts[0] + counts[2] + counts[3] - 1
    stream(0, True)
    push(jnp.minimum(last, 2))
    stream(1, False)
    pop(0, 1)

    def body(step, _):
        stream(0, True)
        pop(1, step - 1)
        push(step + 1)
        stream(1, False)
        pop(0, step)
        return 0

    def finish(part):
        fresh = [pltpu.matmul_pop(unit) for unit in units[part]]
        for start in range(0, half, ROWS):
            rows = slice(start, start + ROWS)
            found = [acc[part][g, rows] for g in range(GROUPS)]
            found[-1] = jnp.maximum(found[-1], jnp.maximum(fresh[0][rows], fresh[1][rows]))
            long, third, fourth = [jnp.maximum(x[:, :LANES], x[:, LANES:]) for x in found]
            lane = lax.broadcasted_iota(jnp.int32, long.shape, 1)
            low = lane < 2 * width
            even = lane // width % 2 == 0
            short = jnp.maximum(
                jnp.where(low, third, fourth),
                pltpu.roll(jnp.where(low, fourth, third), 2 * width, 1),
            )
            best = jnp.maximum(
                jnp.where(even, short, long),
                pltpu.roll(jnp.where(even, long, short), LANES - width, 1),
            )
            partial = best.reshape(ROWS // TOKENS, TOKENS // 8, 8, LANES).sum(axis=1)
            spot = start * 8 // TOKENS
            sums[part, spot : spot + ROWS * 8 // TOKENS] = partial.reshape(-1, LANES)
        total = sums[part, pl.ds(0, half // TOKENS, stride=8), :]
        for k in range(1, 8):
            total = total + sums[part, pl.ds(k, half // TOKENS, stride=8), :]
        write(part, total)

    lax.fori_loop(2, last, body, 0)
    stream(0, True)
    pop(1, last - 1)
    stream(1, False)
    finish(0)
    finish(1)


def score_kernel(first, earlier, rows_of, counts_ref, *refs):
    own_ref, sib_ref, blocks_ref, *refs = refs
    pieces, refs = refs[:earlier], refs[earlier:]
    out_ref, acc_0, acc_1, sums, scores, counts_here, arrived = refs
    load_counts = pltpu.make_async_copy(counts_ref, counts_here, arrived.at[0])
    load_counts.start()
    blocks, rows, dim = blocks_ref.shape
    step = min(blocks - first, BLOCKS)
    local = rows // TOKENS
    half = step * rows // 2
    planes, store, _ = own_ref.shape
    quarter = store // 4
    flat_ref = blocks_ref.reshape(blocks * rows, dim)
    at = sum(piece.shape[0] for piece in pieces)
    waited, placed = [], []

    def row_of(spot):
        return rows_of(lax.axis_index("psg"), spot)

    def receive():
        if placed:
            return
        placed.append(True)
        spot = 0
        for piece in pieces:
            for block in range(piece.shape[0]):
                out_ref[row_of(spot)] = piece[block]
                spot += 1

    def read_counts():
        if not waited:
            waited.append(load_counts.wait())
        return [counts_here[g] for g in range(4)]

    lane = lax.broadcasted_iota(jnp.int32, (16, LANES), 1)
    position = jnp.where(
        lane < store,
        own_ref[planes - 1, :16].astype(jnp.float32),
        sib_ref[planes - 1, :16].astype(jnp.float32) + quarter,
    ).astype(jnp.int32)[:1]

    def run(*units):
        def chunk(start):
            def read_rows(part):
                return flat_ref[pl.ds((first + start) * rows + part * half, half)]

            def write(part, total):
                count = half // TOKENS
                index = jnp.broadcast_to(position, (count, LANES))
                scores[part * count : (part + 1) * count] = jnp.take_along_axis(
                    total, index, axis=1
                )

            score_block(
                own_ref, sib_ref, read_rows, (acc_0, acc_1), sums,
                ((units[0], units[1]), (units[2], units[3])), read_counts, write,
            )
            if earlier:
                receive()
            for block in range(step):
                spot = row_of(at + start + block) if earlier else start + block
                out_ref[spot] = scores[block * local : (block + 1) * local]

        if blocks - first == step:
            chunk(0)
        else:
            read_counts()
            if earlier:
                receive()
            pl.loop(0, blocks - first, step=step)(chunk)

    pl.run_scoped(run, *[pltpu.ACC(unit)((half, 2 * LANES), jnp.float32) for unit in (0, 1, 0, 1)])


def score(counts, own, sib, blocks, first=0, rows_of=None, earlier=()):
    count = blocks.shape[0] - first
    step = min(count, BLOCKS)
    half = step * blocks.shape[1] // 2
    local = blocks.shape[1] // TOKENS
    scalars = [counts]
    operands = [own, sib, blocks, *earlier]
    total = count + sum(piece.shape[0] for piece in earlier)
    held = sum(x.size * x.dtype.itemsize for x in operands) + total * local * LANES * 4
    held += 2 * GROUPS * half * 2 * LANES * 4
    return pl.pallas_call(
        functools.partial(score_kernel, first, len(earlier), rows_of),
        out_shape=jax.ShapeDtypeStruct((total, local, 2 * own.shape[1]), jnp.float32),
        in_specs=[pl.BlockSpec(memory_space=pl.ANY)] * len(scalars) + [VMEM] * len(operands),
        out_specs=VMEM,
        scratch_shapes=[
            pltpu.VMEM((GROUPS, half, 2 * LANES), jnp.float32),
            pltpu.VMEM((GROUPS, half, 2 * LANES), jnp.float32),
            pltpu.VMEM((2, half * 8 // TOKENS, LANES), jnp.float32),
            pltpu.VMEM((step * local, LANES), jnp.float32),
            pltpu.SMEM(counts.shape, jnp.int32),
            pltpu.SemaphoreType.DMA((1,)),
        ],
        compiler_params=pltpu.CompilerParams(vmem_limit_bytes=held + (1 << 20)),
        cost_estimate=pl.CostEstimate(
            flops=8 * count * blocks[0].size * own.shape[0] * own.shape[1],
            bytes_accessed=4 * own.size,
            transcendentals=0,
        ),
        name="score",
    )(*scalars, *operands)


def pick_kernel(core_ref, table_ref, shard_ref, local_ref, out_ref):
    chips, rows, width = table_ref.shape
    store = width // 2
    for half in range(shard_ref.shape[1] // LANES):
        lanes = slice(half * LANES, half * LANES + LANES)
        shard = shard_ref[:, lanes]
        chip = chips - 1 - shard // 2
        lane = ((shard % 2) ^ core_ref[0]) * store + local_ref[:, lanes]
        total = jnp.zeros(lane.shape, jnp.float32)
        for k in range(chips):
            found = jnp.take_along_axis(table_ref[k], lane, axis=1)
            total = jnp.where(chip == k, found, total)
        out_ref[:, lanes] = total


def body(queries, cand_shard, cand_local, passages, lengths):
    core = lax.axis_index("qry").reshape(1).astype(jnp.int32)
    chips = lax.axis_size("psg")
    local, qlen, dim = queries.shape

    def swap(a, bits):
        return lax.ppermute(a, "psg", [(i, i ^ bits) for i in range(chips)])

    own = prep(passages, lengths)
    rows = queries.reshape(1, local * qlen, dim)
    if chips == 16:
        others = [swap(rows, z) for z in (12, 4, 8)]
        own, *others = lax.optimization_barrier((own, *others))
        column = jnp.concatenate([rows] + others, axis=0)
    else:
        column, bit = rows, 4
        while bit < chips:
            column = jnp.concatenate([column, swap(column, bit)], axis=0)
            bit *= 2
    sib = lax.ppermute(own, "qry", [(0, 1), (1, 0)])
    counts = chunk_counts(own, sib)
    near = [0, 12, 4, 8] if chips == 16 else list(range(0, chips, 4))

    def rows_of(chip, spot):
        if isinstance(spot, int):
            return chips - 1 - (chip ^ (near[spot % len(near)] ^ (spot // len(near))))
        return chips - 1 - (chip ^ (spot % len(near) * 4) ^ (spot // len(near)))

    beside = [column] + [swap(column, k) for k in (1, 2, 3)]
    pieces = [score(counts, own, sib, column)]
    pieces += [score(counts, own, sib, beside[k]) for k in (1, 2)]
    table = score(counts, own, sib, beside[3], rows_of=rows_of, earlier=pieces)
    returned = lax.all_to_all(
        table, "psg", split_axis=0, concat_axis=0, tiled=True,
        axis_index_groups=[list(reversed(range(chips)))],
    )
    return pl.pallas_call(
        pick_kernel,
        out_shape=jax.ShapeDtypeStruct(cand_local.shape, jnp.float32),
        in_specs=[SMEM, VMEM, VMEM, VMEM],
        out_specs=VMEM,
        compiler_params=pltpu.CompilerParams(vmem_limit_bytes=4 << 20),
        name="pick",
    )(core, returned, cand_shard[:, :, 0], cand_local)


def solution(mesh):
    in_specs = (
        P(("psg", "qry"), None, None),
        P(("psg", "qry"), None, None),
        P(("psg", "qry"), None),
        P(("psg", "qry"), None, None),
        P(("psg", "qry")),
    )
    out_specs = P(("psg", "qry"), None)
    return jax.shard_map(body, mesh=mesh, in_specs=in_specs, out_specs=out_specs, check_vma=False)
```

```python
import functools

import jax
import jax.numpy as jnp
from jax import lax
from jax.experimental import pallas as pl
from jax.experimental.pallas import tpu as pltpu
from jax.sharding import PartitionSpec as P

VMEM = pl.BlockSpec(memory_space=pltpu.VMEM)
TOKENS = 32
BLOCKS = 4
GROUPS = 3
CHUNK = 8
LANES = 128
ROWS = 128
LOWEST = -1e30


def prep_kernel(counts_ref, store_ref, out_ref, lengths_ref, passages_ref, arrived):
    load_lengths = pltpu.make_async_copy(counts_ref, lengths_ref, arrived.at[0])
    load_store = pltpu.make_async_copy(store_ref, passages_ref, arrived.at[1])
    load_lengths.start()
    load_store.start()
    load_lengths.wait()
    slots, store, dim = passages_ref.shape
    quarter = store // 4
    shape = (store, 2 * store)
    lengths = lengths_ref[...]
    along = jnp.broadcast_to(jnp.concatenate([lengths, lengths], axis=1), shape)
    row = lax.broadcasted_iota(jnp.int32, shape, 0)
    lane = lax.broadcasted_iota(jnp.int32, shape, 1)
    lane = jnp.where(lane >= store, lane - store, lane)
    down = jnp.sum(jnp.where(lane == row, along, 0), axis=1, keepdims=True) // 2
    longer = (down > along) | ((down == along) & (row < lane))
    rank = jnp.sum(longer.astype(jnp.int32), axis=0, keepdims=True)
    sorted_lengths = jnp.sum(jnp.where(rank == row, along, 0), axis=1, keepdims=True) // 2

    square = (2 * store, 2 * store)
    row = lax.broadcasted_iota(jnp.int32, square, 0)
    lane = lax.broadcasted_iota(jnp.int32, square, 1)
    target = rank + jnp.where(lane >= store, store, 0)
    order = (target == row).astype(jnp.float32).astype(passages_ref.dtype)

    load_store.wait()
    first = None
    for t in range(0, slots, 2):
        pair = passages_ref[t : t + 2].reshape(2 * store, dim)
        moved = jnp.dot(order, pair, preferred_element_type=jnp.float32).reshape(2, store, dim)
        first = moved[0] if first is None else first
        for k in range(2):
            out_ref[t + k] = jnp.where(t + k < sorted_lengths, moved[k], first).astype(out_ref.dtype)
    place = rank // quarter
    place = jnp.where(place == 0, 3, jnp.where(place == 1, 1, jnp.where(place == 2, 0, 2)))
    place = place * 2 * quarter + rank % quarter
    for k, value in enumerate((sorted_lengths, place)):
        value = jnp.broadcast_to(value, (store, dim)).astype(jnp.float32)
        out_ref[slots + k] = value.astype(out_ref.dtype)


def prep(passages, lengths):
    store, slots, dim = passages.shape
    return pl.pallas_call(
        prep_kernel,
        out_shape=jax.ShapeDtypeStruct((slots + 2, store, dim), passages.dtype),
        in_specs=[pl.BlockSpec(memory_space=pl.ANY)] * 2,
        out_specs=VMEM,
        scratch_shapes=[
            pltpu.VMEM((1, store), jnp.int32),
            pltpu.VMEM((slots, store, dim), passages.dtype),
            pltpu.SemaphoreType.DMA((2,)),
        ],
        compiler_params=pltpu.CompilerParams(vmem_limit_bytes=4 << 20),
        cost_estimate=pl.CostEstimate(
            flops=64 * passages.size * store, bytes_accessed=4 * passages.size, transcendentals=0
        ),
        name="prep",
    )(
        pltpu.with_memory_space_constraint(lengths.reshape(1, store), pltpu.HBM),
        pltpu.with_memory_space_constraint(passages.transpose(1, 0, 2), pltpu.HBM),
    )


def chunk_counts(own, sib):
    quarter = own.shape[1] // 4
    longest = [plane[-2, ::quarter, 0].astype(jnp.int32) for plane in (own, sib)]
    halves = 2 - (jnp.arange(4, dtype=jnp.int32) >> 1)
    counts = (jnp.maximum(*longest) * halves + 2 * CHUNK - 1) // (2 * CHUNK)
    return jnp.maximum(counts, 2)


def score_block(own_ref, sib_ref, read_rows, acc, sums, units, read_counts, write):
    half = acc[0].shape[1]
    slots = own_ref.shape[0] - 2
    quarter = own_ref.shape[1] // 4
    width = 2 * quarter
    zeros = jnp.zeros((2 * LANES, LANES), own_ref.dtype)

    def where_of(step):
        if isinstance(step, int):
            return 0, step
        third, fourth = counts[0], counts[0] + counts[2]
        group = (step >= third).astype(jnp.int32) + (step >= fourth).astype(jnp.int32)
        start = jnp.where(step >= fourth, fourth, jnp.where(step >= third, third, 0))
        return group, step - start

    def push(step):
        group, at = where_of(step)
        for unit in range(2):
            parts = []
            for k in range(CHUNK):
                token, place = k // 2, (k + k // 2) % 2 * quarter
                slot = at * CHUNK + unit * CHUNK // 2 + token
                if not isinstance(step, int):
                    short = at * 2 * CHUNK + unit * CHUNK + k
                    slot = jnp.minimum(jnp.where(group == 0, slot, short), slots - 1)
                    place = jnp.where(group == 0, place, (group + 1) * quarter)
                    place = pl.multiple_of(place, quarter)
                lanes = pl.ds(place, quarter)
                parts += [own_ref[slot, lanes, :], sib_ref[slot, lanes, :]]
            tile = jnp.concatenate([jnp.concatenate(parts, axis=0), zeros], axis=1)
            pltpu.matmul_push_rhs(tile, 0, unit, transpose=True)

    def stream(part, load):
        rows = read_rows(part)
        rows = jnp.concatenate([rows, jnp.zeros_like(rows)], axis=1)
        for unit in range(2):
            pltpu.matmul_acc_lhs(units[part][unit], rows, 0 if load else None)

    def pop(part, step):
        group, at = where_of(step)
        best = jnp.maximum(pltpu.matmul_pop(units[part][0]), pltpu.matmul_pop(units[part][1]))
        if isinstance(step, int):
            acc[part][group] = best if at == 0 else jnp.maximum(acc[part][group], best)
        else:
            acc[part][group] = jnp.maximum(jnp.where(at == 0, LOWEST, acc[part][group]), best)

    push(0)
    stream(0, True)
    push(1)
    pop(0, 0)
    stream(1, False)
    pop(1, 0)
    counts = read_counts()
    last = counts[0] + counts[2] + counts[3] - 1
    stream(0, True)
    push(jnp.minimum(last, 2))
    stream(1, False)
    pop(0, 1)

    def body(step, _):
        stream(0, True)
        pop(1, step - 1)
        push(step + 1)
        stream(1, False)
        pop(0, step)
        return 0

    def finish(part):
        fresh = [pltpu.matmul_pop(unit) for unit in units[part]]
        for start in range(0, half, ROWS):
            rows = slice(start, start + ROWS)
            found = [acc[part][g, rows] for g in range(GROUPS)]
            found[-1] = jnp.maximum(found[-1], jnp.maximum(fresh[0][rows], fresh[1][rows]))
            long, third, fourth = [jnp.maximum(x[:, :LANES], x[:, LANES:]) for x in found]
            lane = lax.broadcasted_iota(jnp.int32, long.shape, 1)
            low = lane < 2 * width
            even = lane // width % 2 == 0
            short = jnp.maximum(
                jnp.where(low, third, fourth),
                pltpu.roll(jnp.where(low, fourth, third), 2 * width, 1),
            )
            best = jnp.maximum(
                jnp.where(even, short, long),
                pltpu.roll(jnp.where(even, long, short), LANES - width, 1),
            )
            partial = best.reshape(ROWS // TOKENS, TOKENS // 8, 8, LANES).sum(axis=1)
            spot = start * 8 // TOKENS
            sums[part, spot : spot + ROWS * 8 // TOKENS] = partial.reshape(-1, LANES)
        total = sums[part, pl.ds(0, half // TOKENS, stride=8), :]
        for k in range(1, 8):
            total = total + sums[part, pl.ds(k, half // TOKENS, stride=8), :]
        write(part, total)

    lax.fori_loop(2, last, body, 0)
    stream(0, True)
    pop(1, last - 1)
    stream(1, False)
    finish(0)
    finish(1)


def score_kernel(first, earlier, rows_of, counts_ref, *refs):
    own_ref, sib_ref, blocks_ref, *refs = refs
    pieces, refs = refs[:earlier], refs[earlier:]
    out_ref, acc_0, acc_1, sums, scores, counts_here, arrived = refs
    load_counts = pltpu.make_async_copy(counts_ref, counts_here, arrived.at[0])
    load_counts.start()
    blocks, rows, dim = blocks_ref.shape
    step = min(blocks - first, BLOCKS)
    local = rows // TOKENS
    half = step * rows // 2
    planes, store, _ = own_ref.shape
    quarter = store // 4
    flat_ref = blocks_ref.reshape(blocks * rows, dim)
    at = sum(piece.shape[0] for piece in pieces)
    waited, placed = [], []

    def row_of(spot):
        return rows_of(lax.axis_index("psg"), spot)

    def receive():
        if placed:
            return
        placed.append(True)
        spot = 0
        for piece in pieces:
            for block in range(piece.shape[0]):
                out_ref[row_of(spot)] = piece[block]
                spot += 1

    def read_counts():
        if not waited:
            waited.append(load_counts.wait())
        return [counts_here[g] for g in range(4)]

    lane = lax.broadcasted_iota(jnp.int32, (16, LANES), 1)
    position = jnp.where(
        lane < store,
        own_ref[planes - 1, :16].astype(jnp.float32),
        sib_ref[planes - 1, :16].astype(jnp.float32) + quarter,
    ).astype(jnp.int32)[:1]

    def run(*units):
        def chunk(start):
            def read_rows(part):
                return flat_ref[pl.ds((first + start) * rows + part * half, half)]

            def write(part, total):
                count = half // TOKENS
                index = jnp.broadcast_to(position, (count, LANES))
                scores[part * count : (part + 1) * count] = jnp.take_along_axis(
                    total, index, axis=1
                )

            score_block(
                own_ref, sib_ref, read_rows, (acc_0, acc_1), sums,
                ((units[0], units[1]), (units[2], units[3])), read_counts, write,
            )
            if earlier:
                receive()
            for block in range(step):
                spot = row_of(at + start + block) if earlier else start + block
                out_ref[spot] = scores[block * local : (block + 1) * local]

        if blocks - first == step:
            chunk(0)
        else:
            read_counts()
            if earlier:
                receive()
            pl.loop(0, blocks - first, step=step)(chunk)

    pl.run_scoped(run, *[pltpu.ACC(unit)((half, 2 * LANES), jnp.float32) for unit in (0, 1, 0, 1)])


def score(counts, own, sib, blocks, first=0, rows_of=None, earlier=()):
    count = blocks.shape[0] - first
    step = min(count, BLOCKS)
    half = step * blocks.shape[1] // 2
    local = blocks.shape[1] // TOKENS
    scalars = [counts]
    operands = [own, sib, blocks, *earlier]
    total = count + sum(piece.shape[0] for piece in earlier)
    held = sum(x.size * x.dtype.itemsize for x in operands) + total * local * LANES * 4
    held += 2 * GROUPS * half * 2 * LANES * 4
    return pl.pallas_call(
        functools.partial(score_kernel, first, len(earlier), rows_of),
        out_shape=jax.ShapeDtypeStruct((total, local, 2 * own.shape[1]), jnp.float32),
        in_specs=[pl.BlockSpec(memory_space=pl.ANY)] * len(scalars) + [VMEM] * len(operands),
        out_specs=VMEM,
        scratch_shapes=[
            pltpu.VMEM((GROUPS, half, 2 * LANES), jnp.float32),
            pltpu.VMEM((GROUPS, half, 2 * LANES), jnp.float32),
            pltpu.VMEM((2, half * 8 // TOKENS, LANES), jnp.float32),
            pltpu.VMEM((step * local, LANES), jnp.float32),
            pltpu.SMEM(counts.shape, jnp.int32),
            pltpu.SemaphoreType.DMA((1,)),
        ],
        compiler_params=pltpu.CompilerParams(vmem_limit_bytes=held + (1 << 20)),
        cost_estimate=pl.CostEstimate(
            flops=8 * count * blocks[0].size * own.shape[0] * own.shape[1],
            bytes_accessed=4 * own.size,
            transcendentals=0,
        ),
        name="score",
    )(*scalars, *operands)


def pick_kernel(table_ref, shard_ref, local_ref, out_ref):
    chips, rows, width = table_ref.shape
    store = width // 2
    for half in range(shard_ref.shape[1] // LANES):
        lanes = slice(half * LANES, half * LANES + LANES)
        shard = shard_ref[:, lanes]
        chip = chips - 1 - shard // 2
        lane = ((shard % 2) ^ lax.axis_index("qry")) * store + local_ref[:, lanes]
        total = jnp.zeros(lane.shape, jnp.float32)
        for k in range(chips):
            found = jnp.take_along_axis(table_ref[k], lane, axis=1)
            total = jnp.where(chip == k, found, total)
        out_ref[:, lanes] = total


def body(queries, cand_shard, cand_local, passages, lengths):
    chips = lax.axis_size("psg")
    local, qlen, dim = queries.shape

    def swap(a, bits):
        return lax.ppermute(a, "psg", [(i, i ^ bits) for i in range(chips)])

    own = prep(passages, lengths)
    rows = queries.reshape(1, local * qlen, dim)
    if chips == 16:
        others = [swap(rows, z) for z in (12, 4, 8)]
        own, *others = lax.optimization_barrier((own, *others))
        column = jnp.concatenate([rows] + others, axis=0)
    else:
        column, bit = rows, 4
        while bit < chips:
            column = jnp.concatenate([column, swap(column, bit)], axis=0)
            bit *= 2
    sib = lax.ppermute(own, "qry", [(0, 1), (1, 0)])
    counts = chunk_counts(own, sib)
    near = [0, 12, 4, 8] if chips == 16 else list(range(0, chips, 4))

    def rows_of(chip, spot):
        if isinstance(spot, int):
            return chips - 1 - (chip ^ (near[spot % len(near)] ^ (spot // len(near))))
        return chips - 1 - (chip ^ (spot % len(near) * 4) ^ (spot // len(near)))

    beside = [column] + [swap(column, k) for k in (1, 2, 3)]
    pieces = [score(counts, own, sib, column)]
    pieces += [score(counts, own, sib, beside[k]) for k in (1, 2)]
    table = score(counts, own, sib, beside[3], rows_of=rows_of, earlier=pieces)
    returned = lax.all_to_all(
        table, "psg", split_axis=0, concat_axis=0, tiled=True,
        axis_index_groups=[list(reversed(range(chips)))],
    )
    return pl.pallas_call(
        pick_kernel,
        out_shape=jax.ShapeDtypeStruct(cand_local.shape, jnp.float32),
        in_specs=[VMEM, VMEM, VMEM],
        out_specs=VMEM,
        compiler_params=pltpu.CompilerParams(vmem_limit_bytes=4 << 20),
        name="pick",
    )(returned, cand_shard[:, :, 0], cand_local)


def solution(mesh):
    in_specs = (
        P(("psg", "qry"), None, None),
        P(("psg", "qry"), None, None),
        P(("psg", "qry"), None),
        P(("psg", "qry"), None, None),
        P(("psg", "qry")),
    )
    out_specs = P(("psg", "qry"), None)
    return jax.shard_map(body, mesh=mesh, in_specs=in_specs, out_specs=out_specs, check_vma=False)
```
